128 devices in a mesh: pipe: 8 (over x, core), expert: 16 (over z, y).
Axes of the slice: x: 4, y: 4, z: 4, core: 2. Of those that a mesh axis runs over, the one named last changes fastest.
Arguments:
- activations: bfloat16 [1, 2048, 2048], P(None, 'expert'), may hold values from -6 to 6
- norm_gain: bfloat16 [8, 2048], P('pipe'), may hold values from 0.25 to 1.75
- w_gate: bfloat16 [8, 16, 2048, 768], P('pipe', 'expert'), may hold values from -0.125 to 0.125
- w_up: bfloat16 [8, 16, 2048, 768], P('pipe', 'expert'), may hold values from -0.125 to 0.125
- w_down: bfloat16 [8, 16, 768, 2048], P('pipe', 'expert'), may hold values from -0.21875 to 0.21875
- routes: int32 [8, 1, 64, 2], P('pipe', None, 'expert'), may hold values from 0 to 15, as said below
- gate_scores: float32 [8, 1, 64, 2], P('pipe', None, 'expert'), may hold values from 0.25 to 4
Outputs:
- section_out: bfloat16 [8, 1, 2048, 2048], P('pipe', None, 'expert')
The draws below stay inside these ranges and needn't reach their ends.
Inputs may be any that keep to these rules, and one draw needn't show every extreme that they name: `routes`: each entry names an expert. The 2 experts of one block differ. Among the 4 blocks that one device holds for one section and microbatch, no expert is named more than 1 times; in every section and microbatch one expert is named exactly 1 times by the blocks of every device.
All inputs are finite; a program needn't handle non-finite values.
Results may differ from the reference program's by a relative error of at most 0.024.
Values may be sent and summed in bfloat16 or wider, within the bound.
No kernel may reach another device: no remote copies, remote signals or barrier semaphores. Data moves between devices by JAX's collectives and lax.ppermute only.
A program may use at most 64 MiB of HBM per device.

```python
import math
from functools import partial
import jax
import jax.numpy as jnp
from jax import lax

D = 2048
H = 768
TOPK = 2
BLOCK = 32
TOK_DEV = 128
MICRO = 1
EXPERTS = 16
TOKENS = 2048
BLOCKS = 64
SEND = 1
N_PIPE = 8


def device_lookup(key, hot_id, experts_all, blocks_here, send_most):
    key_perm, key_order, key_flip = jax.random.split(key, 3)
    permuted = jax.random.permutation(key_perm, experts_all - 1).astype(jnp.int32)
    others = permuted + (permuted >= hot_id).astype(jnp.int32)
    sequence = others[jnp.arange(2 * blocks_here - send_most) % (experts_all - 1)]
    leading = jnp.stack([jnp.full((send_most,), hot_id, jnp.int32), sequence[:send_most]], 1)
    trailing = sequence[send_most:].reshape(blocks_here - send_most, 2)
    lookup = jnp.concatenate([leading, trailing], 0)
    lookup = lookup[jax.random.permutation(key_order, blocks_here)]
    flipped = jax.random.randint(key_flip, (blocks_here, 1), 0, 2)
    return jnp.where(flipped == 1, lookup[:, ::-1], lookup)


def draw_routes(key, part):
    key = jax.random.fold_in(key, 7)
    groups = N_PIPE * MICRO
    blocks_here = TOK_DEV // BLOCK
    hot_key, device_key = jax.random.split(key)
    hot_ids = jax.random.randint(hot_key, (groups,), 0, EXPERTS).astype(jnp.int32)
    device_keys = jax.random.split(device_key, groups * EXPERTS)
    hot_repeated = jnp.repeat(hot_ids, EXPERTS)
    builder = partial(device_lookup, experts_all=EXPERTS, blocks_here=blocks_here, send_most=SEND)
    lookups = jax.vmap(builder)(device_keys, hot_repeated)
    return lookups.reshape(N_PIPE, MICRO, EXPERTS * blocks_here, TOPK).astype(jnp.int32)


def block_levels(stream_key, dims, cuts, low, top_value):
    gain = 1.0
    for axis_at, parts in cuts:
        draws = jax.random.uniform(jax.random.fold_in(jax.random.fold_in(stream_key, 6), axis_at), (parts,), jnp.float32, low / len(cuts), top_value / len(cuts))
        gain = gain * jnp.repeat(jnp.exp(draws), dims[axis_at] // parts).reshape((-1,) + (1,) * (len(dims) - 1 - axis_at))
    return gain


def gaussian(key, dims, deviation, reach, pieces=(), held_as=jnp.bfloat16):
    array = jax.random.normal(key, dims, jnp.float32) * deviation
    if len(pieces) > 0:
        array = block_levels(key, dims, pieces, -0.22, 0.18) * array
    return jnp.clip(array, min=-reach, max=reach).astype(held_as)


def setup_inputs(seed: int = 0) -> dict:
    splits = jax.random.split(jax.random.key(seed), 8)
    return {
        "activations": gaussian(splits[0], (MICRO, TOKENS, D), 1.0, 6.0, ((1, 16),)),
        "norm_gain": jnp.clip(1.0 + 0.15 * jax.random.normal(splits[1], (N_PIPE, D), jnp.float32), 0.25, 1.75).astype(jnp.bfloat16),
        "w_gate": gaussian(splits[2], (N_PIPE, EXPERTS, D, H), D ** -0.5, 0.125, ((0, 8), (1, 16))),
        "w_up": gaussian(splits[3], (N_PIPE, EXPERTS, D, H), D ** -0.5, 0.125, ((0, 8), (1, 16))),
        "w_down": gaussian(splits[4], (N_PIPE, EXPERTS, H, D), H ** -0.5, 0.21875, ((0, 8), (1, 16))),
        "routes": draw_routes(jax.random.fold_in(splits[7], 71), 0),
        "gate_scores": jnp.clip(jnp.exp(math.log(4.0) - 2.7725887 * jax.random.uniform(splits[6], (N_PIPE, MICRO, BLOCKS, TOPK), jnp.float32) ** block_levels(splits[6], (N_PIPE, MICRO, BLOCKS, TOPK), ((0, 8), (2, 16)), -0.2, 0.2)), 0.25, 4.0),
    }


def one_layer(hidden, gain_row, gate_w, up_w, down_w, route_ids, score_row):
    widened = hidden.astype(jnp.float32)
    scaled = lax.rsqrt(lax.optimization_barrier(jnp.mean(widened * widened, axis=-1, keepdims=True)) + 1e-06)
    normed = (widened * scaled * gain_row.astype(jnp.float32)).astype(jnp.bfloat16)
    block_tiles = normed.reshape(BLOCKS, BLOCK, D)
    chosen = route_ids.reshape(-1)

    def apply_expert(position):
        block_rows = lax.dynamic_index_in_dim(block_tiles, position // TOPK, 0, keepdims=False)
        expert = chosen[position]
        gate_part = jnp.dot(block_rows, gate_w[expert], preferred_element_type=jnp.float32)
        up_part = jnp.dot(block_rows, up_w[expert], preferred_element_type=jnp.float32)
        active = (jax.nn.silu(gate_part) * up_part).astype(jnp.bfloat16)
        return jnp.dot(active, down_w[expert], preferred_element_type=jnp.float32).astype(jnp.bfloat16)
    results = lax.map(apply_expert, jnp.arange(BLOCKS * TOPK, dtype=jnp.int32))
    mix_weight = score_row / lax.optimization_barrier(jnp.sum(score_row, axis=-1, keepdims=True))
    weighted = lax.optimization_barrier(jnp.sum(results.reshape(BLOCKS, TOPK, BLOCK, D).astype(jnp.float32) * mix_weight[:, :, None, None], axis=1))
    return (widened + weighted.reshape(TOKENS, D)).astype(jnp.bfloat16)

def reference(activations, norm_gain, w_gate, w_up, w_down, routes, gate_scores):

    def section_step(carried, section_args):
        gain_row, gate_w, up_w, down_w, route_ids, score_rows = section_args

        def per_micro(micro_args):
            hidden, ids_now, scores_now = micro_args
            return one_layer(hidden, gain_row, gate_w, up_w, down_w, ids_now, scores_now)
        updated = lax.map(per_micro, (carried, route_ids, score_rows))
        return (updated, updated)
    final_state, stacked = lax.scan(section_step, activations, (norm_gain, w_gate, w_up, w_down, routes, gate_scores))
    return stacked
```

```python
import functools

import jax
import jax.numpy as jnp
from jax import lax
from jax.experimental import pallas as pl
from jax.experimental.pallas import tpu as pltpu
from jax.sharding import PartitionSpec as P

VMEM = pltpu.MemorySpace.VMEM
SMEM = pltpu.MemorySpace.SMEM


def normalised(hidden, gain_row):
    scaled = lax.rsqrt(jnp.mean(hidden * hidden, axis=-1, keepdims=True) + 1e-06)
    return (hidden * scaled * gain_row).astype(jnp.bfloat16)


def mixed(hidden_ref, returned_ref, route_ref, score_ref, block):
    topk = route_ref.shape[1]
    scores = [score_ref[block, k] for k in range(topk)]
    whole = scores[0]
    for k in range(1, topk):
        whole = whole + scores[k]
    total = None
    for k in range(topk):
        weight = jnp.full((1, 1), scores[k], jnp.float32) / jnp.full((1, 1), whole, jnp.float32)
        term = returned_ref[route_ref[block, k]].astype(jnp.float32) * weight
        total = term if total is None else total + term
    return (hidden_ref[block].astype(jnp.float32) + total).astype(jnp.bfloat16)


def pack(normed_ref, route_ref, packed_ref):
    blocks, topk = route_ref.shape
    for expert in range(packed_ref.shape[0]):
        block = jnp.int32(0)
        for b in range(1, blocks):
            for k in range(topk):
                block = jnp.where(route_ref[b, k] == expert, jnp.int32(b), block)
        packed_ref[expert] = normed_ref[block]


def enter_kernel(route_ref, hidden_ref, gain_ref, packed_ref, normed_ref):
    for block in range(hidden_ref.shape[0]):
        normed_ref[block] = normalised(hidden_ref[block].astype(jnp.float32), gain_ref[...])
    pack(normed_ref, route_ref, packed_ref)


def between_kernel(
    route_ref, score_ref, next_route_ref, hidden_ref, returned_ref, gain_ref, out_ref, packed_ref, normed_ref
):
    for block in range(hidden_ref.shape[0]):
        result = mixed(hidden_ref, returned_ref, route_ref, score_ref, block)
        out_ref[block] = result
        normed_ref[block] = normalised(result.astype(jnp.float32), gain_ref[...])
    pack(normed_ref, next_route_ref, packed_ref)


def leave_kernel(route_ref, score_ref, hidden_ref, returned_ref, out_ref):
    for block in range(hidden_ref.shape[0]):
        out_ref[block] = mixed(hidden_ref, returned_ref, route_ref, score_ref, block)


def specs(*kinds):
    return [pl.BlockSpec(memory_space={"v": VMEM, "s": SMEM, "a": pl.ANY}[k]) for k in "".join(kinds)]


def enter(routes, hidden, gain, experts):
    blocks, rows, width = hidden.shape
    return pl.pallas_call(
        enter_kernel,
        out_shape=jax.ShapeDtypeStruct((experts, rows, width), jnp.bfloat16),
        in_specs=specs("svv"),
        out_specs=pl.BlockSpec(memory_space=VMEM),
        scratch_shapes=[pltpu.VMEM(hidden.shape, jnp.bfloat16)],
        name="norm_pack",
    )(routes, hidden, gain)


def between(routes, scores, next_routes, hidden, returned, gain):
    return pl.pallas_call(
        between_kernel,
        out_shape=(
            jax.ShapeDtypeStruct(hidden.shape, jnp.bfloat16),
            jax.ShapeDtypeStruct(returned.shape, jnp.bfloat16),
        ),
        in_specs=specs("sssvvv"),
        out_specs=tuple(specs("vv")),
        scratch_shapes=[pltpu.VMEM(hidden.shape, jnp.bfloat16)],
        name="mix_norm_pack",
    )(routes, scores, next_routes, hidden, returned, gain)


def leave(routes, scores, hidden, returned):
    return pl.pallas_call(
        leave_kernel,
        out_shape=jax.ShapeDtypeStruct(hidden.shape, jnp.bfloat16),
        in_specs=specs("ssvv"),
        out_specs=pl.BlockSpec(memory_space=VMEM),
        name="mix",
    )(routes, scores, hidden, returned)


H_CUT = 256
D_CUT = 512


def ffn_kernel(
    pick_ref, x_ref, gate_a, up_a, down_a, gate_b, up_b, down_b, out_ref, gate_v, up_v, down_v, active_v, sems
):
    hidden = gate_v.shape[1]
    width = down_v.shape[1]
    h_parts = hidden // H_CUT
    d_parts = width // D_CUT

    def copies(gate, up, down):
        made = []
        for c in range(h_parts):
            cut = pl.ds(c * H_CUT, H_CUT)
            made.append(pltpu.make_async_copy(gate.at[:, cut], gate_v.at[:, cut], sems.at[2 * c]))
            made.append(pltpu.make_async_copy(up.at[:, cut], up_v.at[:, cut], sems.at[2 * c + 1]))
        for c in range(d_parts):
            cut = pl.ds(c * D_CUT, D_CUT)
            made.append(pltpu.make_async_copy(down.at[:, cut], down_v.at[:, cut], sems.at[2 * h_parts + c]))
        return made

    @pl.when(pick_ref[0] == 0)
    def _():
        for copy in copies(gate_a, up_a, down_a):
            copy.start()

    @pl.when(pick_ref[0] != 0)
    def _():
        for copy in copies(gate_b, up_b, down_b):
            copy.start()

    waits = copies(gate_a, up_a, down_a)
    for c in range(h_parts):
        cut = pl.ds(c * H_CUT, H_CUT)
        waits[2 * c].wait()
        gate_part = jnp.dot(x_ref[...], gate_v[:, cut], preferred_element_type=jnp.float32)
        waits[2 * c + 1].wait()
        up_part = jnp.dot(x_ref[...], up_v[:, cut], preferred_element_type=jnp.float32)
        silu = gate_part / (1.0 + jnp.exp(-gate_part))
        active_v[:, cut] = (silu * up_part).astype(jnp.bfloat16)
    for c in range(d_parts):
        cut = pl.ds(c * D_CUT, D_CUT)
        waits[2 * h_parts + c].wait()
        out_ref[:, cut] = jnp.dot(active_v[...], down_v[:, cut], preferred_element_type=jnp.float32).astype(
            jnp.bfloat16
        )


def ffn(pick, received, first, second):
    experts, rows, width = received.shape
    hidden = first[0].shape[1]
    flat = received.reshape(experts * rows, width)
    count = 2 * (hidden // H_CUT) + width // D_CUT
    produced = pl.pallas_call(
        ffn_kernel,
        out_shape=jax.ShapeDtypeStruct(flat.shape, jnp.bfloat16),
        in_specs=specs("sv", "aaaaaa"),
        out_specs=pl.BlockSpec(memory_space=VMEM),
        scratch_shapes=[
            pltpu.VMEM((width, hidden), jnp.bfloat16),
            pltpu.VMEM((width, hidden), jnp.bfloat16),
            pltpu.VMEM((hidden, width), jnp.bfloat16),
            pltpu.VMEM((flat.shape[0], hidden), jnp.bfloat16),
            pltpu.SemaphoreType.DMA((count,)),
        ],
        compiler_params=pltpu.CompilerParams(vmem_limit_bytes=28 * 1024 * 1024),
        cost_estimate=pl.CostEstimate(
            flops=6 * flat.shape[0] * width * hidden,
            bytes_accessed=6 * width * hidden + 4 * flat.shape[0] * width,
            transcendentals=flat.shape[0] * hidden,
        ),
        name="expert_ffn",
    )(pick, flat, *first, *second)
    return produced.reshape(received.shape)


def exchange(slots):
    return lax.all_to_all(slots, "expert", 0, 0, tiled=True)


def shards(activations, norm_gain, w_gate, w_up, w_down, routes, gate_scores):
    sections = lax.axis_size("pipe")
    experts = lax.axis_size("expert")
    section = lax.axis_index("pipe")
    core = section % 2
    stage = section // 2
    stages = sections // 2
    blocks, topk = routes.shape[2:]
    rows = activations.shape[1] // blocks
    lane = rows // 2
    width = activations.shape[2]
    swap = [(i, i ^ 1) for i in range(sections)]

    own = (w_gate[0, 0], w_up[0, 0], w_down[0, 0])
    small = jnp.concatenate(
        [
            norm_gain[0].astype(jnp.float32),
            routes.reshape(-1).astype(jnp.float32),
            gate_scores.reshape(-1),
            jnp.zeros((128 - 2 * blocks * topk,), jnp.float32),
        ]
    ).reshape(-1, 128)
    other_small = lax.ppermute(small, "pipe", swap)
    other = tuple(lax.ppermute(w, "pipe", swap) for w in own)

    def unpacked(table):
        flat = table.reshape(-1)
        gain = flat[:width].reshape(1, width)
        ids = flat[width : width + blocks * topk].astype(jnp.int32).reshape(blocks, topk)
        scores = flat[width + blocks * topk : width + 2 * blocks * topk].reshape(blocks, topk)
        return gain, ids, scores

    gain_a, route_a, score_a = unpacked(jnp.where(core == 0, small, other_small))
    gain_b, route_b, score_b = unpacked(jnp.where(core == 0, other_small, small))
    pick_a = core.astype(jnp.int32).reshape(1)
    pick_b = 1 - pick_a

    hidden = activations[0].reshape(blocks, 2, lane, width)
    hidden = lax.dynamic_index_in_dim(hidden, core, 1, keepdims=False)
    out_a, out_b = [], []
    for step in range(stages):
        sent = enter(route_a, hidden, gain_a, experts)
        back = exchange(ffn(pick_a, exchange(sent), own, other))
        hidden, sent = between(route_a, score_a, route_b, hidden, back, gain_b)
        out_a.append(hidden)
        back = exchange(ffn(pick_b, exchange(sent), own, other))
        hidden = leave(route_b, score_b, hidden, back)
        out_b.append(hidden)
        if step < stages - 1:
            hidden = lax.ppermute(hidden, "pipe", [(i, i + 2) for i in range(sections - 2)])

    def chosen(values):
        result = values[-1]
        for step in range(stages - 1):
            result = jnp.where(stage == step, values[step], result)
        return result

    result_a, result_b = chosen(out_a), chosen(out_b)
    kept = jnp.where(core == 0, result_a, result_b)
    got = lax.ppermute(jnp.where(core == 0, result_b, result_a), "pipe", swap)
    whole = jnp.where(
        core == 0, jnp.stack([kept, got], axis=1), jnp.stack([got, kept], axis=1)
    )
    return whole.reshape(1, 1, blocks * rows, width)


def solution(mesh):
    in_specs = (
        P(None, "expert", None),
        P("pipe", None),
        P("pipe", "expert", None, None),
        P("pipe", "expert", None, None),
        P("pipe", "expert", None, None),
        P("pipe", None, "expert", None),
        P("pipe", None, "expert", None),
    )
    out_specs = P("pipe", None, "expert", None)
    return jax.shard_map(shards, mesh=mesh, in_specs=in_specs, out_specs=out_specs, check_vma=False)
```

```python
import functools

import jax
import jax.numpy as jnp
from jax import lax
from jax.experimental import pallas as pl
from jax.experimental.pallas import tpu as pltpu
from jax.sharding import PartitionSpec as P

H_CUT = 256
D_CUT = 512
K_CUT = 512
DOWN_PARTS = 3
SMALL = pltpu.CompilerParams(vmem_limit_bytes=8 * 1024 * 1024)


def in_vmem(x):
    return pltpu.with_memory_space_constraint(x, pltpu.VMEM)


def in_hbm(x):
    return pltpu.with_memory_space_constraint(x, pltpu.HBM)


def spec(space):
    return pl.BlockSpec(memory_space=space)


def normalised(hidden, gain_row):
    scaled = lax.rsqrt(jnp.mean(hidden * hidden, axis=-1, keepdims=True) + 1e-06)
    return (hidden * scaled * gain_row).astype(jnp.bfloat16)


def mixed(which, ids_ref, scores_ref, hidden_ref, returned_ref, block):
    topk = ids_ref.shape[1]
    parts = [scores_ref[which, k, block] for k in range(topk)]
    whole = parts[0]
    for k in range(1, topk):
        whole = whole + parts[k]
    total = None
    for k in range(topk):
        weight = jnp.full((1, 1), parts[k], jnp.float32) / jnp.full((1, 1), whole, jnp.float32)
        term = returned_ref[ids_ref[which, k, block]].astype(jnp.float32) * weight
        total = term if total is None else total + term
    return (hidden_ref[block].astype(jnp.float32) + total).astype(jnp.bfloat16)


def pack(ids, normed_ref, packed_ref):
    for expert in range(packed_ref.shape[0]):
        block = jnp.int32(0)
        for b in range(1, len(ids)):
            for one in ids[b]:
                block = jnp.where(one == expert, jnp.int32(b), block)
        packed_ref[expert] = normed_ref[block]


def table_ids(which, ids_ref):
    topk, blocks = ids_ref.shape[1:]
    return [[ids_ref[which, k, b] for k in range(topk)] for b in range(blocks)]


def first_kernel(
    core_ref, ro_h, rx_h, so_h, sx_h, x_hbm, go, gx, gate, up, down,
    hidden_ref, packed_ref, gains_ref, gate_v, up_v, down_v, ids_ref, scores_ref,
    ro, rx, so, sx, normed_ref, gain_v, sems, weight_sems,
):
    core = core_ref[0]
    first = core == 0
    pairs = (
        (ro_h, ro), (rx_h, rx), (so_h, so), (sx_h, sx),
        (go, gain_v.at[0]), (gx, gain_v.at[1]), (x_hbm.at[:, core], hidden_ref),
    )
    copies = [pltpu.make_async_copy(source, target, sems.at[i]) for i, (source, target) in enumerate(pairs)]
    for copy in copies:
        copy.start()
    for copy in copies:
        copy.wait()
    loads = [
        pltpu.make_async_copy(source, target, weight_sems.at[i])
        for i, (source, target) in enumerate(((gate, gate_v), (up, up_v), (down, down_v)))
    ]

    @pl.when(first)
    def _():
        for copy in loads:
            copy.start()

    topk, blocks = ro.shape
    ids = [[None] * topk for _ in range(blocks)]
    for b in range(blocks):
        for k in range(topk):
            ids[b][k] = jnp.where(first, ro[k, b], rx[k, b])
            ids_ref[0, k, b] = ids[b][k]
            ids_ref[1, k, b] = jnp.where(first, rx[k, b], ro[k, b])
            scores_ref[0, k, b] = jnp.where(first, so[k, b], sx[k, b])
            scores_ref[1, k, b] = jnp.where(first, sx[k, b], so[k, b])
    own = gain_v[0].astype(jnp.float32)
    other = gain_v[1].astype(jnp.float32)
    gain = jnp.where(first, own, other)
    gains_ref[0] = gain
    gains_ref[1] = jnp.where(first, other, own)
    for block in range(hidden_ref.shape[0]):
        normed_ref[block] = normalised(hidden_ref[block].astype(jnp.float32), gain)
    pack(ids, normed_ref, packed_ref)

    @pl.when(first)
    def _():
        for copy in loads:
            copy.wait()


def first_call(held, slots, core_table, route, route_x, score, score_x, whole_x, gain, gain_x, own):
    width = held[2]
    both = (2,) + route.shape
    return pl.pallas_call(
        first_kernel,
        out_shape=(
            pltpu.VMEM(held, jnp.bfloat16),
            pltpu.VMEM(slots, jnp.bfloat16),
            pltpu.VMEM((2, 1, width), jnp.float32),
            *[pltpu.VMEM(w.shape, w.dtype) for w in own],
            jax.ShapeDtypeStruct(both, jnp.int32),
            jax.ShapeDtypeStruct(both, jnp.float32),
        ),
        in_specs=[spec(pltpu.SMEM)] + [spec(pltpu.HBM)] * 10,
        out_specs=(spec(pltpu.VMEM),) * 6 + (spec(pltpu.SMEM),) * 2,
        scratch_shapes=[
            pltpu.SMEM(route.shape, jnp.int32),
            pltpu.SMEM(route.shape, jnp.int32),
            pltpu.SMEM(route.shape, jnp.float32),
            pltpu.SMEM(route.shape, jnp.float32),
            pltpu.VMEM(held, jnp.bfloat16),
            pltpu.VMEM((2, 1, width), jnp.bfloat16),
            pltpu.SemaphoreType.DMA((7,)),
            pltpu.SemaphoreType.DMA((3,)),
        ],
        compiler_params=SMALL,
        name="slice_norm_pack",
    )(core_table, *[in_hbm(v) for v in (route, route_x, score, score_x, whole_x, gain, gain_x, *own)])


def enter_kernel(ids_ref, hidden_ref, gains_ref, token_ref, packed_ref, normed_ref):
    del token_ref
    for block in range(hidden_ref.shape[0]):
        normed_ref[block] = normalised(hidden_ref[block].astype(jnp.float32), gains_ref[0])
    pack(table_ids(0, ids_ref), normed_ref, packed_ref)


def between_kernel(ids_ref, scores_ref, hidden_ref, returned_ref, gains_ref, out_ref, packed_ref, normed_ref):
    for block in range(hidden_ref.shape[0]):
        result = mixed(0, ids_ref, scores_ref, hidden_ref, returned_ref, block)
        out_ref[block] = result
        normed_ref[block] = normalised(result.astype(jnp.float32), gains_ref[1])
    pack(table_ids(1, ids_ref), normed_ref, packed_ref)


def leave_kernel(ids_ref, scores_ref, hidden_ref, returned_ref, out_ref, token_ref):
    token_ref[...] = jnp.zeros_like(token_ref)
    for block in range(hidden_ref.shape[0]):
        out_ref[block] = mixed(1, ids_ref, scores_ref, hidden_ref, returned_ref, block)


def small_call(kernel, name, outs, scratch, smem, vmem):
    single = len(outs) == 1
    shapes = tuple(pltpu.VMEM(o, jnp.bfloat16) for o in outs)
    specs = tuple(spec(pltpu.VMEM) for _ in outs)
    return pl.pallas_call(
        kernel,
        out_shape=shapes[0] if single else shapes,
        in_specs=[spec(pltpu.SMEM)] * len(smem) + [spec(pltpu.VMEM)] * len(vmem),
        out_specs=specs[0] if single else specs,
        scratch_shapes=[pltpu.VMEM(s, jnp.bfloat16) for s in scratch],
        compiler_params=SMALL,
        name=name,
    )(*smem, *[in_vmem(v) for v in vmem])


def silu_times(gate_part, up_part):
    return (gate_part / (1.0 + jnp.exp(-gate_part)) * up_part).astype(jnp.bfloat16)


def down_part(active_v, down_ref, out_ref):
    for c in range(down_ref.shape[1] // D_CUT):
        cut = pl.ds(c * D_CUT, D_CUT)
        produced = jnp.dot(active_v[...], down_ref[:, cut], preferred_element_type=jnp.float32)
        out_ref[:, cut] = produced.astype(jnp.bfloat16)


def load_copies(sources, targets, sems):
    (gate, up, down), (gate_ref, up_ref, down_ref) = sources, targets
    parts = gate_ref.shape[0] // K_CUT
    down_rows = down_ref.shape[0] // DOWN_PARTS
    made = []
    for c in range(parts):
        cut = pl.ds(c * K_CUT, K_CUT)
        made.append(pltpu.make_async_copy(gate.at[cut], gate_ref.at[cut], sems.at[2 * c]))
        made.append(pltpu.make_async_copy(up.at[cut], up_ref.at[cut], sems.at[2 * c + 1]))
    for c in range(DOWN_PARTS):
        cut = pl.ds(c * down_rows, down_rows)
        made.append(pltpu.make_async_copy(down.at[cut], down_ref.at[cut], sems.at[2 * parts + c]))
    return made


def streamed_ffn(x_ref, targets, out_ref, active_v, gate_sum, up_sum, waits):
    gate_ref, up_ref, down_ref = targets
    parts = gate_ref.shape[0] // K_CUT
    for c in range(parts):
        cut = pl.ds(c * K_CUT, K_CUT)
        for copy, weight_ref, sum_ref in ((waits[2 * c], gate_ref, gate_sum), (waits[2 * c + 1], up_ref, up_sum)):
            copy.wait()
            term = jnp.dot(x_ref[:, cut], weight_ref[cut, :], preferred_element_type=jnp.float32)
            sum_ref[...] = term if c == 0 else sum_ref[...] + term
    active_v[...] = silu_times(gate_sum[...], up_sum[...])
    for copy in waits[2 * parts :]:
        copy.wait()
    down_part(active_v, down_ref, out_ref)


def first_ffn_kernel(
    core_ref, x_ref, gi, ui, di, gb, ub, db, out_ref, gate_ref, up_ref, down_ref, active_v, gate_sum, up_sum, sems
):
    targets = (gate_ref, up_ref, down_ref)

    @pl.when(core_ref[0] == 0)
    def _():
        ffn_kernel(x_ref, *targets, out_ref, active_v)

    @pl.when(core_ref[0] != 0)
    def _():
        copies = load_copies((gb, ub, db), targets, sems)
        for copy in copies:
            copy.start()
        streamed_ffn(x_ref, targets, out_ref, active_v, gate_sum, up_sum, copies)


def second_ffn_kernel(
    core_ref, x_ref, ga, ua, da, gb, ub, db, out_ref, gate_ref, up_ref, down_ref, active_v, gate_sum, up_sum, sems
):
    targets = (gate_ref, up_ref, down_ref)

    @pl.when(core_ref[0] == 0)
    def _():
        for copy in load_copies((gb, ub, db), targets, sems):
            copy.start()

    @pl.when(core_ref[0] != 0)
    def _():
        for copy in load_copies((ga, ua, da), targets, sems):
            copy.start()

    waits = load_copies((ga, ua, da), targets, sems)
    streamed_ffn(x_ref, targets, out_ref, active_v, gate_sum, up_sum, waits)


def ffn_cost(flat, hidden):
    rows, width = flat.shape
    return pl.CostEstimate(
        flops=6 * rows * width * hidden,
        bytes_accessed=6 * width * hidden + 4 * rows * width,
        transcendentals=rows * hidden,
    )


def load_ffn(kernel, core_table, received, first, second, aliases):
    experts, rows, width = received.shape
    hidden = first[0].shape[1]
    flat = received.reshape(experts * rows, width)
    sums = pltpu.VMEM((flat.shape[0], hidden), jnp.float32)
    place, kind = (in_vmem, pltpu.VMEM) if aliases else (in_hbm, pltpu.HBM)
    produced, *weights = pl.pallas_call(
        kernel,
        out_shape=(pltpu.VMEM(flat.shape, jnp.bfloat16), *[pltpu.VMEM(w.shape, w.dtype) for w in first]),
        in_specs=[spec(pltpu.SMEM), spec(pltpu.VMEM)] + [spec(kind)] * 3 + [spec(pltpu.HBM)] * 3,
        out_specs=(spec(pltpu.VMEM),) * 4,
        scratch_shapes=[
            pltpu.VMEM((flat.shape[0], hidden), jnp.bfloat16),
            sums,
            sums,
            pltpu.SemaphoreType.DMA((2 * (width // K_CUT) + DOWN_PARTS,)),
        ],
        input_output_aliases=aliases,
        compiler_params=SMALL,
        cost_estimate=ffn_cost(flat, hidden),
        name="load_expert_ffn",
    )(core_table, in_vmem(flat), *[place(w) for w in first], *[in_hbm(w) for w in second])
    return produced.reshape(received.shape), weights


def ffn_kernel(x_ref, gate_ref, up_ref, down_ref, out_ref, active_v):
    for c in range(gate_ref.shape[1] // H_CUT):
        cut = pl.ds(c * H_CUT, H_CUT)
        gate_part = jnp.dot(x_ref[...], gate_ref[:, cut], preferred_element_type=jnp.float32)
        up_part = jnp.dot(x_ref[...], up_ref[:, cut], preferred_element_type=jnp.float32)
        active_v[:, cut] = silu_times(gate_part, up_part)
    down_part(active_v, down_ref, out_ref)


def ffn(received, weights):
    experts, rows, width = received.shape
    hidden = weights[0].shape[1]
    flat = received.reshape(experts * rows, width)
    produced = pl.pallas_call(
        ffn_kernel,
        out_shape=pltpu.VMEM(flat.shape, jnp.bfloat16),
        in_specs=[spec(pltpu.VMEM)] * 4,
        out_specs=spec(pltpu.VMEM),
        scratch_shapes=[pltpu.VMEM((flat.shape[0], hidden), jnp.bfloat16)],
        compiler_params=SMALL,
        cost_estimate=ffn_cost(flat, hidden),
        name="expert_ffn",
    )(in_vmem(flat), *[in_vmem(w) for w in weights])
    return produced.reshape(received.shape)


def exchange(slots):
    return lax.all_to_all(slots, "expert", 0, 0, tiled=True)


def shards(activations, norm_gain, w_gate, w_up, w_down, routes, gate_scores):
    sections = lax.axis_size("pipe")
    experts = lax.axis_size("expert")
    section = lax.axis_index("pipe")
    core = section % 2
    stage = section // 2
    stages = sections // 2
    blocks, topk = routes.shape[2:]
    rows = activations.shape[1] // blocks
    lane = rows // 2
    width = activations.shape[2]
    held = (blocks, lane, width)
    slots = (experts, lane, width)
    swap = [(i, i ^ 1) for i in range(sections)]

    def swapped(x):
        return lax.ppermute(x, "pipe", swap)

    route = routes[0, 0].T
    score = gate_scores[0, 0].T
    route_x, gain_x, score_x = swapped(route), swapped(norm_gain), swapped(score)
    own = (w_gate[0, 0], w_up[0, 0], w_down[0, 0])
    *own, route_x, gain_x, score_x = lax.optimization_barrier((*own, route_x, gain_x, score_x))
    other = tuple(swapped(w) for w in own)
    core_table = core.astype(jnp.int32).reshape(1)

    whole_x = activations[0].reshape(blocks, 2, lane, width)
    hidden, sent, gains, *weights_a, ids, scores = first_call(
        held, slots, core_table, route, route_x, score, score_x, whole_x, norm_gain, gain_x, own
    )
    out_a, out_b = [], []
    for step in range(stages):
        if step == 0:
            made, weights_a = load_ffn(
                first_ffn_kernel, core_table, exchange(sent), weights_a, other, {2: 1, 3: 2, 4: 3}
            )
        else:
            made = ffn(exchange(sent), weights_a)
        hidden, sent = small_call(
            between_kernel, "mix_norm_pack", (held, slots), (held,), (ids, scores), (hidden, exchange(made), gains)
        )
        out_a.append(hidden)
        if step == 0:
            made, weights_b = load_ffn(second_ffn_kernel, core_table, exchange(sent), own, other, {})
        else:
            made = ffn(exchange(sent), weights_b)
        hidden, token = small_call(
            leave_kernel, "mix", (held, (16, 128)), (), (ids, scores), (hidden, exchange(made))
        )
        out_b.append(hidden)
        if step < stages - 1:
            hidden = lax.ppermute(hidden, "pipe", [(i, i + 2) for i in range(sections - 2)])
            if step > 0:
                token = lax.ppermute(token, "pipe", [(i, i + 1) for i in range(0, sections, 2)])
            sent = small_call(enter_kernel, "norm_pack", (slots,), (held,), (ids,), (hidden, gains, token))

    def chosen(values):
        result = values[-1]
        for step in range(stages - 1):
            result = jnp.where(stage == step, values[step], result)
        return result

    result_a, result_b = chosen(out_a), chosen(out_b)
    kept = jnp.where(core == 0, result_a, result_b)
    got = swapped(jnp.where(core == 0, result_b, result_a))
    whole = jnp.where(core == 0, jnp.stack([kept, got], axis=1), jnp.stack([got, kept], axis=1))
    return whole.reshape(1, 1, blocks * rows, width)


def solution(mesh):
    in_specs = (
        P(None, "expert", None),
        P("pipe", None),
        P("pipe", "expert", None, None),
        P("pipe", "expert", None, None),
        P("pipe", "expert", None, None),
        P("pipe", None, "expert", None),
        P("pipe", None, "expert", None),
    )
    out_specs = P("pipe", None, "expert", None)
    return jax.shard_map(shards, mesh=mesh, in_specs=in_specs, out_specs=out_specs, check_vma=False)
```

```python
import functools

import jax
import jax.numpy as jnp
from jax import lax
from jax.experimental import pallas as pl
from jax.experimental.pallas import tpu as pltpu
from jax.sharding import PartitionSpec as P

H_CUT = 256
D_CUT = 512
HELD = (1,)
K_CUT = 512
DOWN_PARTS = 3
SMALL = pltpu.CompilerParams(vmem_limit_bytes=8 * 1024 * 1024)


def in_vmem(x):
    return pltpu.with_memory_space_constraint(x, pltpu.VMEM)


def in_hbm(x):
    return pltpu.with_memory_space_constraint(x, pltpu.HBM)


def spec(space):
    return pl.BlockSpec(memory_space=space)


def core_of(section_ref):
    return section_ref[0] & 1


def normalised(hidden, gain_row):
    scaled = lax.rsqrt(jnp.mean(hidden * hidden, axis=-1, keepdims=True) + 1e-06)
    return (hidden * scaled * gain_row).astype(jnp.bfloat16)


def mixed(which, ids_ref, scores_ref, hidden_ref, returned_ref, block):
    topk = ids_ref.shape[1]
    parts = [scores_ref[which, k, block] for k in range(topk)]
    whole = parts[0]
    for k in range(1, topk):
        whole = whole + parts[k]
    total = None
    for k in range(topk):
        weight = jnp.full((1, 1), parts[k], jnp.float32) / jnp.full((1, 1), whole, jnp.float32)
        term = returned_ref[ids_ref[which, k, block]].astype(jnp.float32) * weight
        total = term if total is None else total + term
    return (hidden_ref[block].astype(jnp.float32) + total).astype(jnp.bfloat16)


def pack(ids, normed_ref, packed_ref):
    for expert in range(packed_ref.shape[0]):
        block = jnp.int32(0)
        for b in range(1, len(ids)):
            for one in ids[b]:
                block = jnp.where(one == expert, jnp.int32(b), block)
        packed_ref[expert] = normed_ref[block]


def table_ids(which, ids_ref):
    topk, blocks = ids_ref.shape[1:]
    return [[ids_ref[which, k, b] for k in range(topk)] for b in range(blocks)]


def first_kernel(
    section_ref, rx_h, sx_h, gx, ro_h, so_h, go, x_hbm, gate, up, down,
    hidden_ref, packed_ref, gains_ref, gate_v, up_v, down_v, ids_ref, scores_ref,
    ro, rx, so, sx, normed_ref, gain_v, sems, weight_sems,
):
    core = core_of(section_ref)
    first = core == 0
    pairs = (
        (ro_h, ro), (rx_h, rx), (so_h, so), (sx_h, sx),
        (go, gain_v.at[0]), (gx, gain_v.at[1]), (x_hbm.at[:, core], hidden_ref),
    )
    copies = [pltpu.make_async_copy(source, target, sems.at[i]) for i, (source, target) in enumerate(pairs)]
    for copy in copies:
        copy.start()
    for copy in copies:
        copy.wait()
    loads = [
        pltpu.make_async_copy(source, target, weight_sems.at[i])
        for i, (source, target) in enumerate(((gate, gate_v), (up, up_v), (down, down_v)))
    ]

    topk, blocks = ro.shape
    ids = [[None] * topk for _ in range(blocks)]
    for b in range(blocks):
        for k in range(topk):
            ids[b][k] = jnp.where(first, ro[k, b], rx[k, b])
            ids_ref[0, k, b] = ids[b][k]
            ids_ref[1, k, b] = jnp.where(first, rx[k, b], ro[k, b])
            scores_ref[0, k, b] = jnp.where(first, so[k, b], sx[k, b])
            scores_ref[1, k, b] = jnp.where(first, sx[k, b], so[k, b])
    own = gain_v[0].astype(jnp.float32)
    other = gain_v[1].astype(jnp.float32)
    gain = jnp.where(first, own, other)
    gains_ref[0] = gain
    gains_ref[1] = jnp.where(first, other, own)
    for block in range(hidden_ref.shape[0]):
        normed_ref[block] = normalised(hidden_ref[block].astype(jnp.float32), gain)
    pack(ids, normed_ref, packed_ref)

    @pl.when(first)
    def _():
        for copy in loads:
            copy.start()
        for copy in loads:
            copy.wait()


def first_call(held, slots, section_table, route, route_x, score, score_x, whole_x, gain, gain_x, own):
    width = held[2]
    both = (2,) + route.shape
    return pl.pallas_call(
        first_kernel,
        out_shape=(
            pltpu.VMEM(held, jnp.bfloat16),
            pltpu.VMEM(slots, jnp.bfloat16),
            pltpu.VMEM((2, 1, width), jnp.float32),
            *[pltpu.VMEM(w.shape, w.dtype) for w in own],
            jax.ShapeDtypeStruct(both, jnp.int32),
            jax.ShapeDtypeStruct(both, jnp.float32),
        ),
        in_specs=[spec(pltpu.SMEM)] + [spec(pl.ANY)] * 3 + [spec(pltpu.HBM)] * 7,
        out_specs=(spec(pltpu.VMEM),) * 6 + (spec(pltpu.SMEM),) * 2,
        scratch_shapes=[
            pltpu.SMEM(route.shape, jnp.int32),
            pltpu.SMEM(route.shape, jnp.int32),
            pltpu.SMEM(route.shape, jnp.float32),
            pltpu.SMEM(route.shape, jnp.float32),
            pltpu.VMEM(held, jnp.bfloat16),
            pltpu.VMEM((2, 1, width), jnp.bfloat16),
            pltpu.SemaphoreType.DMA((7,)),
            pltpu.SemaphoreType.DMA((3,)),
        ],
        compiler_params=SMALL,
        name="slice_norm_pack",
    )(section_table, route_x, score_x, gain_x, *[in_hbm(v) for v in (route, score, gain, whole_x, *own)])


def enter_kernel(ids_ref, hidden_ref, gains_ref, *refs):
    packed_ref, normed_ref = refs[-2:]
    for block in range(hidden_ref.shape[0]):
        normed_ref[block] = normalised(hidden_ref[block].astype(jnp.float32), gains_ref[0])
    pack(table_ids(0, ids_ref), normed_ref, packed_ref)


def between_kernel(ids_ref, scores_ref, hidden_ref, returned_ref, gains_ref, out_ref, packed_ref, normed_ref):
    for block in range(hidden_ref.shape[0]):
        result = mixed(0, ids_ref, scores_ref, hidden_ref, returned_ref, block)
        out_ref[block] = result
        normed_ref[block] = normalised(result.astype(jnp.float32), gains_ref[1])
    pack(table_ids(1, ids_ref), normed_ref, packed_ref)


def leave_kernel(ids_ref, scores_ref, hidden_ref, returned_ref, out_ref, token_ref):
    token_ref[...] = jnp.zeros_like(token_ref)
    for block in range(hidden_ref.shape[0]):
        out_ref[block] = mixed(1, ids_ref, scores_ref, hidden_ref, returned_ref, block)


def finish_kernel(section_ref, ids_ref, scores_ref, hidden_ref, returned_ref, *refs):
    earlier, (kept_ref, sent_ref, last_ref, sems) = refs[:-4], refs[-4:]
    stages = (len(earlier) + 1) // 2
    for block in range(hidden_ref.shape[0]):
        last_ref[block] = mixed(1, ids_ref, scores_ref, hidden_ref, returned_ref, block)
    results_a, results_b = earlier[:stages], (*earlier[stages:], last_ref)
    for step in range(stages):
        for core, targets in ((0, (kept_ref, sent_ref)), (1, (sent_ref, kept_ref))):

            @pl.when(section_ref[0] == 2 * step + core)
            def _():
                for i, source in enumerate((results_a[step], results_b[step])):
                    pltpu.make_async_copy(source, targets[i], sems.at[i]).start()

    for i, target in enumerate((kept_ref, sent_ref)):
        pltpu.make_async_copy(results_a[0], target, sems.at[i]).wait()


def finish(section_table, ids, scores, hidden, returned, earlier):
    held = hidden.shape
    return pl.pallas_call(
        finish_kernel,
        out_shape=(pltpu.VMEM(held, jnp.bfloat16),) * 2,
        in_specs=[spec(pltpu.SMEM)] * 3 + [spec(pltpu.VMEM)] * 2 + [spec(pl.ANY)] * len(earlier),
        out_specs=(spec(pltpu.VMEM),) * 2,
        scratch_shapes=[pltpu.VMEM(held, jnp.bfloat16), pltpu.SemaphoreType.DMA((2,))],
        compiler_params=SMALL,
        name="mix_choose",
    )(section_table, ids, scores, in_vmem(hidden), in_vmem(returned), *earlier)


def join_kernel(section_ref, kept_ref, got_ref, out_ref, sems):
    copies = [
        pltpu.make_async_copy(kept_ref, out_ref.at[:, core_of(section_ref)], sems.at[0]),
        pltpu.make_async_copy(got_ref, out_ref.at[:, 1 - core_of(section_ref)], sems.at[1]),
    ]
    for copy in copies:
        copy.start()
    for copy in copies:
        copy.wait()


def join(section_table, kept, got):
    blocks, lane, width = kept.shape
    return pl.pallas_call(
        join_kernel,
        out_shape=pltpu.HBM((blocks, 2, lane, width), jnp.bfloat16),
        in_specs=[spec(pltpu.SMEM)] + [spec(pltpu.VMEM)] * 2,
        out_specs=spec(pltpu.HBM),
        scratch_shapes=[pltpu.SemaphoreType.DMA((2,))],
        compiler_params=SMALL,
        name="join_rows",
    )(section_table, in_vmem(kept), in_vmem(got))


def small_call(kernel, name, outs, scratch, smem, vmem):
    single = len(outs) == 1
    shapes = tuple(pltpu.VMEM(o, jnp.bfloat16) for o in outs)
    specs = tuple(spec(pltpu.VMEM) for _ in outs)
    return pl.pallas_call(
        kernel,
        out_shape=shapes[0] if single else shapes,
        in_specs=[spec(pltpu.SMEM)] * len(smem) + [spec(pltpu.VMEM)] * len(vmem),
        out_specs=specs[0] if single else specs,
        scratch_shapes=[pltpu.VMEM(s, jnp.bfloat16) for s in scratch],
        compiler_params=SMALL,
        name=name,
    )(*smem, *[in_vmem(v) for v in vmem])


def silu_times(gate_part, up_part):
    return (gate_part / (1.0 + jnp.exp(-gate_part)) * up_part).astype(jnp.bfloat16)


def down_part(active_v, down_ref, out_ref):
    for c in range(down_ref.shape[1] // D_CUT):
        cut = pl.ds(c * D_CUT, D_CUT)
        produced = jnp.dot(active_v[...], down_ref[:, cut], preferred_element_type=jnp.float32)
        out_ref[:, cut] = produced.astype(jnp.bfloat16)


def load_copies(sources, targets, sems):
    (gate, up, down), (gate_ref, up_ref, down_ref) = sources, targets
    parts = gate_ref.shape[0] // K_CUT
    down_rows = down_ref.shape[0] // DOWN_PARTS
    made = []
    for c in range(parts):
        cut = pl.ds(c * K_CUT, K_CUT)
        made.append(pltpu.make_async_copy(gate.at[cut], gate_ref.at[cut], sems.at[2 * c]))
        made.append(pltpu.make_async_copy(up.at[cut], up_ref.at[cut], sems.at[2 * c + 1]))
    for c in range(DOWN_PARTS):
        cut = pl.ds(c * down_rows, down_rows)
        made.append(pltpu.make_async_copy(down.at[cut], down_ref.at[cut], sems.at[2 * parts + c]))
    return made


def streamed_ffn(x_ref, targets, out_ref, active_v, gate_sum, up_sum, down_sum, waits):
    gate_ref, up_ref, down_ref = targets
    parts = gate_ref.shape[0] // K_CUT
    for c in range(parts):
        cut = pl.ds(c * K_CUT, K_CUT)
        for copy, weight_ref, sum_ref in ((waits[2 * c], gate_ref, gate_sum), (waits[2 * c + 1], up_ref, up_sum)):
            copy.wait()
            term = jnp.dot(x_ref[:, cut], weight_ref[cut, :], preferred_element_type=jnp.float32)
            sum_ref[...] = term if c == 0 else sum_ref[...] + term
    active_v[...] = silu_times(gate_sum[...], up_sum[...])
    down_rows = down_ref.shape[0] // DOWN_PARTS
    for c in range(DOWN_PARTS):
        waits[2 * parts + c].wait()
        cut = pl.ds(c * down_rows, down_rows)
        term = jnp.dot(active_v[:, cut], down_ref[cut, :], preferred_element_type=jnp.float32)
        if c == 0:
            down_sum[...] = term
        elif c < DOWN_PARTS - 1:
            down_sum[...] += term
        else:
            out_ref[...] = (down_sum[...] + term).astype(jnp.bfloat16)


def first_ffn_kernel(
    section_ref, x_ref, gi, ui, di, gb, ub, db, out_ref, gate_ref, up_ref, down_ref, active_v, gate_sum, up_sum, down_sum, sems
):
    targets = (gate_ref, up_ref, down_ref)

    @pl.when(core_of(section_ref) == 0)
    def _():
        ffn_kernel(x_ref, *targets, out_ref, active_v)

    @pl.when(core_of(section_ref) != 0)
    def _():
        copies = load_copies((gb, ub, db), targets, sems)
        for copy in copies:
            copy.start()
        streamed_ffn(x_ref, targets, out_ref, active_v, gate_sum, up_sum, down_sum, copies)


def second_ffn_kernel(
    section_ref, x_ref, ga, ua, da, gb, ub, db, out_ref, gate_ref, up_ref, down_ref, active_v, gate_sum, up_sum, down_sum, sems
):
    targets = (gate_ref, up_ref, down_ref)

    @pl.when(core_of(section_ref) == 0)
    def _():
        for copy in load_copies((gb, ub, db), targets, sems):
            copy.start()

    @pl.when(core_of(section_ref) != 0)
    def _():
        for copy in load_copies((ga, ua, da), targets, sems):
            copy.start()

    waits = load_copies((ga, ua, da), targets, sems)
    streamed_ffn(x_ref, targets, out_ref, active_v, gate_sum, up_sum, down_sum, waits)


def ffn_cost(flat, hidden):
    rows, width = flat.shape
    return pl.CostEstimate(
        flops=6 * rows * width * hidden,
        bytes_accessed=6 * width * hidden + 4 * rows * width,
        transcendentals=rows * hidden,
    )


def load_ffn(kernel, section_table, received, first, second, aliases):
    experts, rows, width = received.shape
    hidden = first[0].shape[1]
    flat = received.reshape(experts * rows, width)
    sums = pltpu.VMEM((flat.shape[0], hidden), jnp.float32)
    place, kind = (in_vmem, pltpu.VMEM) if aliases else (in_hbm, pltpu.HBM)
    produced, *weights = pl.pallas_call(
        kernel,
        out_shape=(pltpu.VMEM(flat.shape, jnp.bfloat16), *[pltpu.VMEM(w.shape, w.dtype) for w in first]),
        in_specs=[spec(pltpu.SMEM), spec(pltpu.VMEM)] + [spec(kind)] * 3 + [spec(pl.ANY)] * 3,
        out_specs=(spec(pltpu.VMEM),) * 4,
        scratch_shapes=[
            pltpu.VMEM((flat.shape[0], hidden), jnp.bfloat16),
            sums,
            sums,
            pltpu.VMEM(flat.shape, jnp.float32),
            pltpu.SemaphoreType.DMA((2 * (width // K_CUT) + DOWN_PARTS,)),
        ],
        input_output_aliases=aliases,
        compiler_params=SMALL,
        cost_estimate=ffn_cost(flat, hidden),
        name="load_expert_ffn",
    )(section_table, in_vmem(flat), *[place(w) for w in first], *second)
    return produced.reshape(received.shape), weights


def ffn_kernel(x_ref, gate_ref, up_ref, down_ref, out_ref, active_v):
    for c in range(gate_ref.shape[1] // H_CUT):
        cut = pl.ds(c * H_CUT, H_CUT)
        gate_part = jnp.dot(x_ref[...], gate_ref[:, cut], preferred_element_type=jnp.float32)
        up_part = jnp.dot(x_ref[...], up_ref[:, cut], preferred_element_type=jnp.float32)
        active_v[:, cut] = silu_times(gate_part, up_part)
    down_part(active_v, down_ref, out_ref)


def ffn(received, weights):
    experts, rows, width = received.shape
    hidden = weights[0].shape[1]
    flat = received.reshape(experts * rows, width)
    produced = pl.pallas_call(
        ffn_kernel,
        out_shape=pltpu.VMEM(flat.shape, jnp.bfloat16),
        in_specs=[spec(pltpu.VMEM)] * 4,
        out_specs=spec(pltpu.VMEM),
        scratch_shapes=[pltpu.VMEM((flat.shape[0], hidden), jnp.bfloat16)],
        compiler_params=SMALL,
        cost_estimate=ffn_cost(flat, hidden),
        name="expert_ffn",
    )(in_vmem(flat), *[in_vmem(w) for w in weights])
    return produced.reshape(received.shape)


def exchange(slots):
    return lax.all_to_all(slots, "expert", 0, 0, tiled=True)


def shards(activations, norm_gain, w_gate, w_up, w_down, routes, gate_scores):
    sections = lax.axis_size("pipe")
    experts = lax.axis_size("expert")
    section = lax.axis_index("pipe")
    stages = sections // 2
    blocks, topk = routes.shape[2:]
    rows = activations.shape[1] // blocks
    lane = rows // 2
    width = activations.shape[2]
    held = (blocks, lane, width)
    slots = (experts, lane, width)
    swap = [(i, i ^ 1) for i in range(sections)]

    def swapped(x):
        return lax.ppermute(x, "pipe", swap)

    route = routes[0, 0].T
    score = gate_scores[0, 0].T
    route_x, gain_x, score_x = swapped(route), swapped(norm_gain), swapped(score)
    own = (w_gate[0, 0], w_up[0, 0], w_down[0, 0])
    *own, route_x, gain_x, score_x = lax.optimization_barrier((*own, route_x, gain_x, score_x))
    other = tuple(swapped(w) for w in own)
    section_table = section.astype(jnp.int32).reshape(1)

    whole_x = activations[0].reshape(blocks, 2, lane, width)
    hidden, sent, gains, *weights_a, ids, scores = first_call(
        held, slots, section_table, route, route_x, score, score_x, whole_x, norm_gain, gain_x, own
    )
    out_a, out_b = [], []
    for step in range(stages):
        if step == 0:
            made, weights_a = load_ffn(
                first_ffn_kernel, section_table, exchange(sent), weights_a, other, {2: 1, 3: 2, 4: 3}
            )
        else:
            made = ffn(exchange(sent), weights_a)
        hidden, sent = small_call(
            between_kernel, "mix_norm_pack", (held, slots), (held,), (ids, scores), (hidden, exchange(made), gains)
        )
        out_a.append(hidden)
        if step == 0:
            made, weights_b = load_ffn(second_ffn_kernel, section_table, exchange(sent), own, other, {})
        else:
            made = ffn(exchange(sent), weights_b)
        back = exchange(made)
        if step == stages - 1:
            break
        hidden, token = small_call(leave_kernel, "mix", (held, (16, 128)), (), (ids, scores), (hidden, back))
        out_b.append(hidden)
        hidden = lax.ppermute(hidden, "pipe", [(i, (i + 2) % sections) for i in range(sections)])
        tokens = ()
        if step in HELD:
            tokens = (lax.ppermute(token, "pipe", [(i, i + 1) for i in range(0, sections, 2)]),)
        sent = small_call(enter_kernel, "norm_pack", (slots,), (held,), (ids,), (hidden, gains, *tokens))

    kept, leaving = finish(section_table, ids, scores, hidden, back, out_a + out_b)
    whole = join(section_table, kept, swapped(leaving))
    return whole.reshape(1, 1, blocks * rows, width)


def solution(mesh):
    in_specs = (
        P(None, "expert", None),
        P("pipe", None),
        P("pipe", "expert", None, None),
        P("pipe", "expert", None, None),
        P("pipe", "expert", None, None),
        P("pipe", None, "expert", None),
        P("pipe", None, "expert", None),
    )
    out_specs = P("pipe", None, "expert", None)
    return jax.shard_map(shards, mesh=mesh, in_specs=in_specs, out_specs=out_specs, check_vma=False)
```

```python
import functools

import jax
import jax.numpy as jnp
from jax import lax
from jax.experimental import pallas as pl
from jax.experimental.pallas import tpu as pltpu
from jax.sharding import PartitionSpec as P

H_CUT = 256
D_CUT = 512
HELD = (1,)
K_CUT = 512
DOWN_PARTS = 3
SMALL = pltpu.CompilerParams(vmem_limit_bytes=8 * 1024 * 1024)


def in_vmem(x):
    return pltpu.with_memory_space_constraint(x, pltpu.VMEM)


def in_hbm(x):
    return pltpu.with_memory_space_constraint(x, pltpu.HBM)


def spec(space):
    return pl.BlockSpec(memory_space=space)


def core_of(section_ref):
    return section_ref[0] & 1


def normalised(hidden, gain_row):
    scaled = lax.rsqrt(jnp.mean(hidden * hidden, axis=-1, keepdims=True) + 1e-06)
    return (hidden * scaled * gain_row).astype(jnp.bfloat16)


def mixed(which, ids_ref, scores_ref, hidden_ref, returned_ref, block):
    topk = ids_ref.shape[1]
    parts = [scores_ref[which, k, block] for k in range(topk)]
    whole = parts[0]
    for k in range(1, topk):
        whole = whole + parts[k]
    total = None
    for k in range(topk):
        weight = jnp.full((1, 1), parts[k], jnp.float32) / jnp.full((1, 1), whole, jnp.float32)
        term = returned_ref[ids_ref[which, k, block]].astype(jnp.float32) * weight
        total = term if total is None else total + term
    return (hidden_ref[block].astype(jnp.float32) + total).astype(jnp.bfloat16)


def pack(ids, normed_ref, packed_ref):
    for expert in range(packed_ref.shape[0]):
        block = jnp.int32(0)
        for b in range(1, len(ids)):
            for one in ids[b]:
                block = jnp.where(one == expert, jnp.int32(b), block)
        packed_ref[expert] = normed_ref[block]


def table_ids(which, ids_ref):
    topk, blocks = ids_ref.shape[1:]
    return [[ids_ref[which, k, b] for k in range(topk)] for b in range(blocks)]


def first_kernel(
    section_ref, rx_h, sx_h, gx, ro_h, so_h, go, x_hbm, gate, up, down,
    hidden_ref, packed_ref, gains_ref, gate_v, up_v, down_v, ids_ref, scores_ref,
    ro, rx, so, sx, normed_ref, gain_v, sems, weight_sems,
):
    core = core_of(section_ref)
    first = core == 0
    pairs = (
        (ro_h, ro), (rx_h, rx), (so_h, so), (sx_h, sx),
        (go, gain_v.at[0]), (gx, gain_v.at[1]), (x_hbm.at[:, core], hidden_ref),
    )
    copies = [pltpu.make_async_copy(source, target, sems.at[i]) for i, (source, target) in enumerate(pairs)]
    for copy in copies:
        copy.start()
    for copy in copies:
        copy.wait()
    loads = [
        pltpu.make_async_copy(source, target, weight_sems.at[i])
        for i, (source, target) in enumerate(((gate, gate_v), (up, up_v), (down, down_v)))
    ]

    topk, blocks = ro.shape
    ids = [[None] * topk for _ in range(blocks)]
    for b in range(blocks):
        for k in range(topk):
            ids[b][k] = jnp.where(first, ro[k, b], rx[k, b])
            ids_ref[0, k, b] = ids[b][k]
            ids_ref[1, k, b] = jnp.where(first, rx[k, b], ro[k, b])
            scores_ref[0, k, b] = jnp.where(first, so[k, b], sx[k, b])
            scores_ref[1, k, b] = jnp.where(first, sx[k, b], so[k, b])
    own = gain_v[0].astype(jnp.float32)
    other = gain_v[1].astype(jnp.float32)
    gain = jnp.where(first, own, other)
    gains_ref[0] = gain
    gains_ref[1] = jnp.where(first, other, own)
    for block in range(hidden_ref.shape[0]):
        normed_ref[block] = normalised(hidden_ref[block].astype(jnp.float32), gain)
    pack(ids, normed_ref, packed_ref)

    @pl.when(first)
    def _():
        for copy in loads:
            copy.start()
        for copy in loads:
            copy.wait()


def first_call(held, slots, section_table, route, route_x, score, score_x, whole_x, gain, gain_x, own):
    width = held[2]
    both = (2,) + route.shape
    return pl.pallas_call(
        first_kernel,
        out_shape=(
            pltpu.VMEM(held, jnp.bfloat16),
            pltpu.VMEM(slots, jnp.bfloat16),
            pltpu.VMEM((2, 1, width), jnp.float32),
            *[pltpu.VMEM(w.shape, w.dtype) for w in own],
            pltpu.SMEM(both, jnp.int32),
            pltpu.SMEM(both, jnp.float32),
        ),
        in_specs=[spec(pltpu.SMEM)] + [spec(pl.ANY)] * 3 + [spec(pltpu.HBM)] * 7,
        out_specs=(spec(pltpu.VMEM),) * 6 + (spec(pltpu.SMEM),) * 2,
        scratch_shapes=[
            pltpu.SMEM(route.shape, jnp.int32),
            pltpu.SMEM(route.shape, jnp.int32),
            pltpu.SMEM(route.shape, jnp.float32),
            pltpu.SMEM(route.shape, jnp.float32),
            pltpu.VMEM(held, jnp.bfloat16),
            pltpu.VMEM((2, 1, width), jnp.bfloat16),
            pltpu.SemaphoreType.DMA((7,)),
            pltpu.SemaphoreType.DMA((3,)),
        ],
        compiler_params=SMALL,
        name="slice_norm_pack",
    )(section_table, route_x, score_x, gain_x, *[in_hbm(v) for v in (route, score, gain, whole_x, *own)])


def enter_kernel(ids_ref, hidden_ref, gains_ref, *refs):
    packed_ref, normed_ref = refs[-2:]
    for block in range(hidden_ref.shape[0]):
        normed_ref[block] = normalised(hidden_ref[block].astype(jnp.float32), gains_ref[0])
    pack(table_ids(0, ids_ref), normed_ref, packed_ref)


def between_kernel(ids_ref, scores_ref, hidden_ref, returned_ref, gains_ref, out_ref, packed_ref, normed_ref):
    for block in range(hidden_ref.shape[0]):
        result = mixed(0, ids_ref, scores_ref, hidden_ref, returned_ref, block)
        out_ref[block] = result
        normed_ref[block] = normalised(result.astype(jnp.float32), gains_ref[1])
    pack(table_ids(1, ids_ref), normed_ref, packed_ref)


def leave_kernel(ids_ref, scores_ref, hidden_ref, returned_ref, out_ref, *token_refs):
    for token_ref in token_refs:
        token_ref[...] = jnp.zeros_like(token_ref)
    for block in range(hidden_ref.shape[0]):
        out_ref[block] = mixed(1, ids_ref, scores_ref, hidden_ref, returned_ref, block)


def finish_kernel(section_ref, ids_ref, scores_ref, hidden_ref, returned_ref, *refs):
    earlier, (kept_ref, sent_ref, last_ref, sems) = refs[:-4], refs[-4:]
    stages = (len(earlier) + 1) // 2
    for block in range(hidden_ref.shape[0]):
        last_ref[block] = mixed(1, ids_ref, scores_ref, hidden_ref, returned_ref, block)
    results_a, results_b = earlier[:stages], (*earlier[stages:], last_ref)
    for step in range(stages):
        for core, targets in ((0, (kept_ref, sent_ref)), (1, (sent_ref, kept_ref))):

            @pl.when(section_ref[0] == 2 * step + core)
            def _():
                for i, source in enumerate((results_a[step], results_b[step])):
                    pltpu.make_async_copy(source, targets[i], sems.at[i]).start()

    for i, target in enumerate((kept_ref, sent_ref)):
        pltpu.make_async_copy(results_a[0], target, sems.at[i]).wait()


def finish(section_table, ids, scores, hidden, returned, earlier):
    held = hidden.shape
    return pl.pallas_call(
        finish_kernel,
        out_shape=(pltpu.VMEM(held, jnp.bfloat16),) * 2,
        in_specs=[spec(pltpu.SMEM)] * 3 + [spec(pltpu.VMEM)] * 2 + [spec(pl.ANY)] * len(earlier),
        out_specs=(spec(pltpu.VMEM),) * 2,
        scratch_shapes=[pltpu.VMEM(held, jnp.bfloat16), pltpu.SemaphoreType.DMA((2,))],
        compiler_params=SMALL,
        name="mix_choose",
    )(section_table, ids, scores, in_vmem(hidden), in_vmem(returned), *earlier)


def join_kernel(section_ref, kept_ref, got_ref, out_ref, sems):
    copies = [
        pltpu.make_async_copy(kept_ref, out_ref.at[:, core_of(section_ref)], sems.at[0]),
        pltpu.make_async_copy(got_ref, out_ref.at[:, 1 - core_of(section_ref)], sems.at[1]),
    ]
    for copy in copies:
        copy.start()
    for copy in copies:
        copy.wait()


def join(section_table, kept, got):
    blocks, lane, width = kept.shape
    return pl.pallas_call(
        join_kernel,
        out_shape=pltpu.HBM((blocks, 2, lane, width), jnp.bfloat16),
        in_specs=[spec(pltpu.SMEM)] + [spec(pltpu.VMEM)] * 2,
        out_specs=spec(pltpu.HBM),
        scratch_shapes=[pltpu.SemaphoreType.DMA((2,))],
        compiler_params=SMALL,
        name="join_rows",
    )(section_table, in_vmem(kept), in_vmem(got))


def small_call(kernel, name, outs, scratch, smem, vmem):
    single = len(outs) == 1
    shapes = tuple(pltpu.VMEM(o, jnp.bfloat16) for o in outs)
    specs = tuple(spec(pltpu.VMEM) for _ in outs)
    return pl.pallas_call(
        kernel,
        out_shape=shapes[0] if single else shapes,
        in_specs=[spec(pltpu.SMEM)] * len(smem) + [spec(pltpu.VMEM)] * len(vmem),
        out_specs=specs[0] if single else specs,
        scratch_shapes=[pltpu.VMEM(s, jnp.bfloat16) for s in scratch],
        compiler_params=SMALL,
        name=name,
    )(*smem, *[in_vmem(v) for v in vmem])


def silu_times(gate_part, up_part):
    return (gate_part / (1.0 + jnp.exp(-gate_part)) * up_part).astype(jnp.bfloat16)


def down_part(active_v, down_ref, out_ref):
    for c in range(down_ref.shape[1] // D_CUT):
        cut = pl.ds(c * D_CUT, D_CUT)
        produced = jnp.dot(active_v[...], down_ref[:, cut], preferred_element_type=jnp.float32)
        out_ref[:, cut] = produced.astype(jnp.bfloat16)


def load_copies(sources, targets, sems):
    (gate, up, down), (gate_ref, up_ref, down_ref) = sources, targets
    parts = gate_ref.shape[0] // K_CUT
    down_rows = down_ref.shape[0] // DOWN_PARTS
    made = []
    for c in range(parts):
        cut = pl.ds(c * K_CUT, K_CUT)
        made.append(pltpu.make_async_copy(gate.at[cut], gate_ref.at[cut], sems.at[2 * c]))
        made.append(pltpu.make_async_copy(up.at[cut], up_ref.at[cut], sems.at[2 * c + 1]))
    for c in range(DOWN_PARTS):
        cut = pl.ds(c * down_rows, down_rows)
        made.append(pltpu.make_async_copy(down.at[cut], down_ref.at[cut], sems.at[2 * parts + c]))
    return made


def streamed_ffn(x_ref, targets, out_ref, active_v, gate_sum, up_sum, down_sum, waits):
    gate_ref, up_ref, down_ref = targets
    parts = gate_ref.shape[0] // K_CUT
    for c in range(parts):
        cut = pl.ds(c * K_CUT, K_CUT)
        for copy, weight_ref, sum_ref in ((waits[2 * c], gate_ref, gate_sum), (waits[2 * c + 1], up_ref, up_sum)):
            copy.wait()
            term = jnp.dot(x_ref[:, cut], weight_ref[cut, :], preferred_element_type=jnp.float32)
            sum_ref[...] = term if c == 0 else sum_ref[...] + term
    active_v[...] = silu_times(gate_sum[...], up_sum[...])
    down_rows = down_ref.shape[0] // DOWN_PARTS
    for c in range(DOWN_PARTS):
        waits[2 * parts + c].wait()
        cut = pl.ds(c * down_rows, down_rows)
        term = jnp.dot(active_v[:, cut], down_ref[cut, :], preferred_element_type=jnp.float32)
        if c == 0:
            down_sum[...] = term
        elif c < DOWN_PARTS - 1:
            down_sum[...] += term
        else:
            out_ref[...] = (down_sum[...] + term).astype(jnp.bfloat16)


def first_ffn_kernel(
    section_ref, x_ref, gi, ui, di, gx, ux, dx, out_ref, gate_ref, up_ref, down_ref, gate_next, up_next, down_next,
    active_v, gate_sum, up_sum, down_sum, sems
):
    @pl.when(core_of(section_ref) == 0)
    def _():
        copies = load_copies((gx, ux, dx), (gate_next, up_next, down_next), sems)
        for copy in copies:
            copy.start()
        ffn_kernel(x_ref, gate_ref, up_ref, down_ref, out_ref, active_v)
        for copy in copies:
            copy.wait()

    @pl.when(core_of(section_ref) != 0)
    def _():
        stream_and_run(x_ref, (gx, ux, dx), (gate_ref, up_ref, down_ref), out_ref, active_v,
                       gate_sum, up_sum, down_sum, sems)


def second_ffn_kernel(
    section_ref, x_ref, gi, ui, di, g_h, u_h, d_h, out_ref, gate_ref, up_ref, down_ref,
    active_v, gate_sum, up_sum, down_sum, sems
):
    @pl.when(core_of(section_ref) == 0)
    def _():
        ffn_kernel(x_ref, gate_ref, up_ref, down_ref, out_ref, active_v)

    @pl.when(core_of(section_ref) != 0)
    def _():
        stream_and_run(x_ref, (g_h, u_h, d_h), (gate_ref, up_ref, down_ref), out_ref, active_v,
                       gate_sum, up_sum, down_sum, sems)


def stream_and_run(x_ref, sources, targets, out_ref, active_v, gate_sum, up_sum, down_sum, sems):
    copies = load_copies(sources, targets, sems)
    for copy in copies:
        copy.start()
    streamed_ffn(x_ref, targets, out_ref, active_v, gate_sum, up_sum, down_sum, copies)


def ffn_cost(flat, hidden):
    rows, width = flat.shape
    return pl.CostEstimate(
        flops=6 * rows * width * hidden,
        bytes_accessed=6 * width * hidden + 4 * rows * width,
        transcendentals=rows * hidden,
    )


def load_ffn(kernel, section_table, received, present, sources, extra):
    experts, rows, width = received.shape
    hidden = present[0].shape[1]
    flat = received.reshape(experts * rows, width)
    sums = pltpu.VMEM((flat.shape[0], hidden), jnp.float32)
    produced, *weights = pl.pallas_call(
        kernel,
        out_shape=(
            pltpu.VMEM(flat.shape, jnp.bfloat16),
            *[pltpu.VMEM(w.shape, w.dtype) for w in present] * (1 + extra),
        ),
        in_specs=[spec(pltpu.SMEM)] + [spec(pltpu.VMEM)] * 4 + [spec(pl.ANY if extra else pltpu.HBM)] * 3,
        out_specs=(spec(pltpu.VMEM),) * (4 + 3 * extra),
        scratch_shapes=[
            pltpu.VMEM((flat.shape[0], hidden), jnp.bfloat16),
            sums,
            sums,
            pltpu.VMEM(flat.shape, jnp.float32),
            pltpu.SemaphoreType.DMA((2 * (width // K_CUT) + DOWN_PARTS,)),
        ],
        input_output_aliases={2: 1, 3: 2, 4: 3},
        compiler_params=SMALL,
        cost_estimate=ffn_cost(flat, hidden),
        name="load_expert_ffn",
    )(
        section_table,
        in_vmem(flat),
        *[in_vmem(w) for w in present],
        *(sources if extra else [in_hbm(w) for w in sources]),
    )
    return produced.reshape(received.shape), weights


def ffn_kernel(x_ref, gate_ref, up_ref, down_ref, out_ref, active_v):
    for c in range(gate_ref.shape[1] // H_CUT):
        cut = pl.ds(c * H_CUT, H_CUT)
        gate_part = jnp.dot(x_ref[...], gate_ref[:, cut], preferred_element_type=jnp.float32)
        up_part = jnp.dot(x_ref[...], up_ref[:, cut], preferred_element_type=jnp.float32)
        active_v[:, cut] = silu_times(gate_part, up_part)
    down_part(active_v, down_ref, out_ref)


def ffn(received, weights):
    experts, rows, width = received.shape
    hidden = weights[0].shape[1]
    flat = received.reshape(experts * rows, width)
    produced = pl.pallas_call(
        ffn_kernel,
        out_shape=pltpu.VMEM(flat.shape, jnp.bfloat16),
        in_specs=[spec(pltpu.VMEM)] * 4,
        out_specs=spec(pltpu.VMEM),
        scratch_shapes=[pltpu.VMEM((flat.shape[0], hidden), jnp.bfloat16)],
        compiler_params=SMALL,
        cost_estimate=ffn_cost(flat, hidden),
        name="expert_ffn",
    )(in_vmem(flat), *[in_vmem(w) for w in weights])
    return produced.reshape(received.shape)


def exchange(slots):
    return lax.all_to_all(slots, "expert", 0, 0, tiled=True)


def shards(activations, norm_gain, w_gate, w_up, w_down, routes, gate_scores):
    sections = lax.axis_size("pipe")
    experts = lax.axis_size("expert")
    section = lax.axis_index("pipe")
    stages = sections // 2
    blocks, topk = routes.shape[2:]
    rows = activations.shape[1] // blocks
    lane = rows // 2
    width = activations.shape[2]
    held = (blocks, lane, width)
    slots = (experts, lane, width)
    swap = [(i, i ^ 1) for i in range(sections)]

    def swapped(x):
        return lax.ppermute(x, "pipe", swap)

    route = routes[0, 0].T
    score = gate_scores[0, 0].T
    route_x, gain_x, score_x = swapped(route), swapped(norm_gain), swapped(score)
    own = (w_gate[0, 0], w_up[0, 0], w_down[0, 0])
    *own, route_x, gain_x, score_x = lax.optimization_barrier((*own, route_x, gain_x, score_x))
    other = tuple(swapped(w) for w in own)
    section_table = section.astype(jnp.int32).reshape(1)

    whole_x = activations[0].reshape(blocks, 2, lane, width)
    hidden, sent, gains, *weights_a, ids, scores = first_call(
        held, slots, section_table, route, route_x, score, score_x, whole_x, norm_gain, gain_x, own
    )
    out_a, out_b = [], []
    for step in range(stages):
        if step == 0:
            made, weights = load_ffn(first_ffn_kernel, section_table, exchange(sent), weights_a, other, 1)
            weights_a, weights_b = weights[:3], weights[3:]
        else:
            made = ffn(exchange(sent), weights_a)
        hidden, sent = small_call(
            between_kernel, "mix_norm_pack", (held, slots), (held,), (ids, scores), (hidden, exchange(made), gains)
        )
        out_a.append(hidden)
        if step == 0:
            made, weights_b = load_ffn(second_ffn_kernel, section_table, exchange(sent), weights_b, own, 0)
        else:
            made = ffn(exchange(sent), weights_b)
        back = exchange(made)
        if step == stages - 1:
            break
        outs = (held, (16, 128)) if step in HELD else (held,)
        left = small_call(leave_kernel, "mix", outs, (), (ids, scores), (hidden, back))
        hidden, tokens = (left[0], left[1:]) if step in HELD else (left, ())
        out_b.append(hidden)
        hidden = lax.ppermute(hidden, "pipe", [(i, (i + 2) % sections) for i in range(sections)])
        tokens = [lax.ppermute(t, "pipe", [(i, i + 1) for i in range(0, sections, 2)]) for t in tokens]
        sent = small_call(enter_kernel, "norm_pack", (slots,), (held,), (ids,), (hidden, gains, *tokens))

    kept, leaving = finish(section_table, ids, scores, hidden, back, out_a + out_b)
    whole = join(section_table, kept, swapped(leaving))
    return whole.reshape(1, 1, blocks * rows, width)


def solution(mesh):
    in_specs = (
        P(None, "expert", None),
        P("pipe", None),
        P("pipe", "expert", None, None),
        P("pipe", "expert", None, None),
        P("pipe", "expert", None, None),
        P("pipe", None, "expert", None),
        P("pipe", None, "expert", None),
    )
    out_specs = P("pipe", None, "expert", None)
    return jax.shard_map(shards, mesh=mesh, in_specs=in_specs, out_specs=out_specs, check_vma=False)
```

```python
import functools

import jax
import jax.numpy as jnp
from jax import lax
from jax.experimental import pallas as pl
from jax.experimental.pallas import tpu as pltpu
from jax.sharding import PartitionSpec as P

H_CUT = 256
D_CUT = 512
STREAM, LOAD = 1, 2
CORE_1 = ((STREAM, STREAM), (STREAM, LOAD), (LOAD, STREAM), (LOAD, LOAD))
AHEAD = 8
K_CUT = 512
DOWN_PARTS = 3
SMALL = pltpu.CompilerParams(vmem_limit_bytes=8 * 1024 * 1024)


def in_vmem(x):
    return pltpu.with_memory_space_constraint(x, pltpu.VMEM)


def in_hbm(x):
    return pltpu.with_memory_space_constraint(x, pltpu.HBM)


def spec(space):
    return pl.BlockSpec(memory_space=space)


def core_of(section_ref):
    return section_ref[0] & 1


def normalised(hidden, gain_row):
    scaled = lax.rsqrt(jnp.mean(hidden * hidden, axis=-1, keepdims=True) + 1e-06)
    return (hidden * scaled * gain_row).astype(jnp.bfloat16)


def mixed(which, ids_ref, scores_ref, hidden_ref, returned_ref, block):
    topk = ids_ref.shape[1]
    parts = [scores_ref[which, k, block] for k in range(topk)]
    whole = parts[0]
    for k in range(1, topk):
        whole = whole + parts[k]
    total = None
    for k in range(topk):
        weight = jnp.full((1, 1), parts[k], jnp.float32) / jnp.full((1, 1), whole, jnp.float32)
        term = returned_ref[ids_ref[which, k, block]].astype(jnp.float32) * weight
        total = term if total is None else total + term
    return (hidden_ref[block].astype(jnp.float32) + total).astype(jnp.bfloat16)


def pack(ids, normed_ref, packed_ref):
    for expert in range(packed_ref.shape[0]):
        block = jnp.int32(0)
        for b in range(1, len(ids)):
            for one in ids[b]:
                block = jnp.where(one == expert, jnp.int32(b), block)
        packed_ref[expert] = normed_ref[block]


def table_ids(which, ids_ref):
    topk, blocks = ids_ref.shape[1:]
    return [[ids_ref[which, k, b] for k in range(topk)] for b in range(blocks)]


def first_kernel(
    section_ref, rx_h, sx_h, gx, ro_h, so_h, go, x_hbm, gate, up, down,
    hidden_ref, packed_ref, gains_ref, gate_v, up_v, down_v, ids_ref, scores_ref,
    ro, rx, so, sx, normed_ref, gain_v, sems, weight_sems,
):
    core = core_of(section_ref)
    first = core == 0
    pairs = (
        (ro_h, ro), (rx_h, rx), (so_h, so), (sx_h, sx),
        (go, gain_v.at[0]), (gx, gain_v.at[1]), (x_hbm.at[:, core], hidden_ref),
    )
    copies = [pltpu.make_async_copy(source, target, sems.at[i]) for i, (source, target) in enumerate(pairs)]
    for copy in copies:
        copy.start()
    for copy in copies:
        copy.wait()
    loads = [
        pltpu.make_async_copy(source, target, weight_sems.at[i])
        for i, (source, target) in enumerate(((gate, gate_v), (up, up_v), (down, down_v)))
    ]

    topk, blocks = ro.shape
    ids = [[None] * topk for _ in range(blocks)]
    for b in range(blocks):
        for k in range(topk):
            ids[b][k] = jnp.where(first, ro[k, b], rx[k, b])
            ids_ref[0, k, b] = ids[b][k]
            ids_ref[1, k, b] = jnp.where(first, rx[k, b], ro[k, b])
            scores_ref[0, k, b] = jnp.where(first, so[k, b], sx[k, b])
            scores_ref[1, k, b] = jnp.where(first, sx[k, b], so[k, b])
    own = gain_v[0].astype(jnp.float32)
    other = gain_v[1].astype(jnp.float32)
    gain = jnp.where(first, own, other)
    gains_ref[0] = gain
    gains_ref[1] = jnp.where(first, other, own)
    for block in range(hidden_ref.shape[0]):
        normed_ref[block] = normalised(hidden_ref[block].astype(jnp.float32), gain)
    pack(ids, normed_ref, packed_ref)

    @pl.when(first)
    def _():
        for copy in loads:
            copy.start()
        for copy in loads:
            copy.wait()


def first_call(held, slots, section_table, route, route_x, score, score_x, whole_x, gain, gain_x, own):
    width = held[2]
    both = (2,) + route.shape
    return pl.pallas_call(
        first_kernel,
        out_shape=(
            pltpu.VMEM(held, jnp.bfloat16),
            pltpu.VMEM(slots, jnp.bfloat16),
            pltpu.VMEM((2, 1, width), jnp.float32),
            *[pltpu.VMEM(w.shape, w.dtype) for w in own],
            pltpu.SMEM(both, jnp.int32),
            pltpu.SMEM(both, jnp.float32),
        ),
        in_specs=[spec(pltpu.SMEM)] + [spec(pl.ANY)] * 3 + [spec(pltpu.HBM)] * 7,
        out_specs=(spec(pltpu.VMEM),) * 6 + (spec(pltpu.SMEM),) * 2,
        scratch_shapes=[
            pltpu.SMEM(route.shape, jnp.int32),
            pltpu.SMEM(route.shape, jnp.int32),
            pltpu.SMEM(route.shape, jnp.float32),
            pltpu.SMEM(route.shape, jnp.float32),
            pltpu.VMEM(held, jnp.bfloat16),
            pltpu.VMEM((2, 1, width), jnp.bfloat16),
            pltpu.SemaphoreType.DMA((7,)),
            pltpu.SemaphoreType.DMA((3,)),
        ],
        compiler_params=SMALL,
        name="slice_norm_pack",
    )(section_table, route_x, score_x, gain_x, *[in_hbm(v) for v in (route, score, gain, whole_x, *own)])


def enter_kernel(ids_ref, hidden_ref, gains_ref, packed_ref, normed_ref):
    for block in range(hidden_ref.shape[0]):
        normed_ref[block] = normalised(hidden_ref[block].astype(jnp.float32), gains_ref[0])
    pack(table_ids(0, ids_ref), normed_ref, packed_ref)


def between_kernel(ids_ref, scores_ref, hidden_ref, returned_ref, gains_ref, out_ref, packed_ref, normed_ref):
    for block in range(hidden_ref.shape[0]):
        result = mixed(0, ids_ref, scores_ref, hidden_ref, returned_ref, block)
        out_ref[block] = result
        normed_ref[block] = normalised(result.astype(jnp.float32), gains_ref[1])
    pack(table_ids(1, ids_ref), normed_ref, packed_ref)


def leave_kernel(ids_ref, scores_ref, hidden_ref, returned_ref, out_ref):
    for block in range(hidden_ref.shape[0]):
        out_ref[block] = mixed(1, ids_ref, scores_ref, hidden_ref, returned_ref, block)


def finish_kernel(section_ref, ids_ref, scores_ref, hidden_ref, returned_ref, *refs):
    earlier, (kept_ref, sent_ref, last_ref, sems) = refs[:-4], refs[-4:]
    stages = (len(earlier) + 1) // 2
    for block in range(hidden_ref.shape[0]):
        last_ref[block] = mixed(1, ids_ref, scores_ref, hidden_ref, returned_ref, block)
    results_a, results_b = earlier[:stages], (*earlier[stages:], last_ref)
    for step in range(stages):
        for core, targets in ((0, (kept_ref, sent_ref)), (1, (sent_ref, kept_ref))):

            @pl.when(section_ref[0] == 2 * step + core)
            def _():
                for i, source in enumerate((results_a[step], results_b[step])):
                    pltpu.make_async_copy(source, targets[i], sems.at[i]).start()

    for i, target in enumerate((kept_ref, sent_ref)):
        pltpu.make_async_copy(results_a[0], target, sems.at[i]).wait()


def finish(section_table, ids, scores, hidden, returned, earlier):
    held = hidden.shape
    return pl.pallas_call(
        finish_kernel,
        out_shape=(pltpu.VMEM(held, jnp.bfloat16),) * 2,
        in_specs=[spec(pltpu.SMEM)] * 3 + [spec(pltpu.VMEM)] * 2 + [spec(pl.ANY)] * len(earlier),
        out_specs=(spec(pltpu.VMEM),) * 2,
        scratch_shapes=[pltpu.VMEM(held, jnp.bfloat16), pltpu.SemaphoreType.DMA((2,))],
        compiler_params=SMALL,
        name="mix_choose",
    )(section_table, ids, scores, in_vmem(hidden), in_vmem(returned), *earlier)


def join_kernel(section_ref, kept_ref, got_ref, out_ref, sems):
    copies = [
        pltpu.make_async_copy(kept_ref, out_ref.at[:, core_of(section_ref)], sems.at[0]),
        pltpu.make_async_copy(got_ref, out_ref.at[:, 1 - core_of(section_ref)], sems.at[1]),
    ]
    for copy in copies:
        copy.start()
    for copy in copies:
        copy.wait()


def join(section_table, kept, got):
    blocks, lane, width = kept.shape
    return pl.pallas_call(
        join_kernel,
        out_shape=pltpu.HBM((blocks, 2, lane, width), jnp.bfloat16),
        in_specs=[spec(pltpu.SMEM)] + [spec(pltpu.VMEM)] * 2,
        out_specs=spec(pltpu.HBM),
        scratch_shapes=[pltpu.SemaphoreType.DMA((2,))],
        compiler_params=SMALL,
        name="join_rows",
    )(section_table, in_vmem(kept), in_vmem(got))


def small_call(kernel, name, outs, scratch, smem, vmem):
    single = len(outs) == 1
    shapes = tuple(pltpu.VMEM(o, jnp.bfloat16) for o in outs)
    specs = tuple(spec(pltpu.VMEM) for _ in outs)
    return pl.pallas_call(
        kernel,
        out_shape=shapes[0] if single else shapes,
        in_specs=[spec(pltpu.SMEM)] * len(smem) + [spec(pltpu.VMEM)] * len(vmem),
        out_specs=specs[0] if single else specs,
        scratch_shapes=[pltpu.VMEM(s, jnp.bfloat16) for s in scratch],
        compiler_params=SMALL,
        name=name,
    )(*smem, *[in_vmem(v) for v in vmem])


def silu_times(gate_part, up_part):
    return (gate_part / (1.0 + jnp.exp(-gate_part)) * up_part).astype(jnp.bfloat16)


def down_part(active_v, down_ref, out_ref):
    for c in range(down_ref.shape[1] // D_CUT):
        cut = pl.ds(c * D_CUT, D_CUT)
        produced = jnp.dot(active_v[...], down_ref[:, cut], preferred_element_type=jnp.float32)
        out_ref[:, cut] = produced.astype(jnp.bfloat16)


def load_copies(sources, targets, sems):
    (gate, up, down), (gate_ref, up_ref, down_ref) = sources, targets
    parts = gate_ref.shape[0] // K_CUT
    down_rows = down_ref.shape[0] // DOWN_PARTS
    made = []
    for c in range(parts):
        cut = pl.ds(c * K_CUT, K_CUT)
        made.append(pltpu.make_async_copy(gate.at[cut], gate_ref.at[cut], sems.at[2 * c]))
        made.append(pltpu.make_async_copy(up.at[cut], up_ref.at[cut], sems.at[2 * c + 1]))
    for c in range(DOWN_PARTS):
        cut = pl.ds(c * down_rows, down_rows)
        made.append(pltpu.make_async_copy(down.at[cut], down_ref.at[cut], sems.at[2 * parts + c]))
    return made


def streamed_ffn(x_ref, targets, out_ref, active_v, gate_sum, up_sum, down_sum, waits):
    gate_ref, up_ref, down_ref = targets
    parts = gate_ref.shape[0] // K_CUT
    for c in range(parts):
        cut = pl.ds(c * K_CUT, K_CUT)
        for copy, weight_ref, sum_ref in ((waits[2 * c], gate_ref, gate_sum), (waits[2 * c + 1], up_ref, up_sum)):
            copy.wait()
            term = jnp.dot(x_ref[:, cut], weight_ref[cut, :], preferred_element_type=jnp.float32)
            sum_ref[...] = term if c == 0 else sum_ref[...] + term
    active_v[...] = silu_times(gate_sum[...], up_sum[...])
    down_rows = down_ref.shape[0] // DOWN_PARTS
    for c in range(DOWN_PARTS):
        waits[2 * parts + c].wait()
        cut = pl.ds(c * down_rows, down_rows)
        term = jnp.dot(active_v[:, cut], down_ref[cut, :], preferred_element_type=jnp.float32)
        if c == 0:
            down_sum[...] = term
        elif c < DOWN_PARTS - 1:
            down_sum[...] += term
        else:
            out_ref[...] = (down_sum[...] + term).astype(jnp.bfloat16)


def first_ffn_kernel(
    section_ref, x_ref, gi, ui, di, gx, ux, dx, out_ref, gate_ref, up_ref, down_ref, gate_next, up_next, down_next,
    active_v, gate_sum, up_sum, down_sum, sems
):
    @pl.when(core_of(section_ref) == 0)
    def _():
        copies = load_copies((gx, ux, dx), (gate_next, up_next, down_next), sems)
        for copy in copies:
            copy.start()
        for copy in copies[:AHEAD]:
            copy.wait()
        ffn_kernel(x_ref, gate_ref, up_ref, down_ref, out_ref, active_v)
        for copy in copies[AHEAD:]:
            copy.wait()

    @pl.when(core_of(section_ref) != 0)
    def _():
        stream_and_run(x_ref, (gx, ux, dx), (gate_ref, up_ref, down_ref), out_ref, active_v,
                       gate_sum, up_sum, down_sum, sems)


def second_ffn_kernel(
    way, section_ref, x_ref, gi, ui, di, g_h, u_h, d_h, out_ref, gate_ref, up_ref, down_ref,
    active_v, gate_sum, up_sum, down_sum, sems
):
    @pl.when(core_of(section_ref) == 0)
    def _():
        ffn_kernel(x_ref, gate_ref, up_ref, down_ref, out_ref, active_v)

    @pl.when(core_of(section_ref) != 0)
    def _():
        sources, targets = (g_h, u_h, d_h), (gate_ref, up_ref, down_ref)
        if way == STREAM:
            stream_and_run(x_ref, sources, targets, out_ref, active_v, gate_sum, up_sum, down_sum, sems)
        else:
            copies = load_copies(sources, targets, sems)
            for copy in copies:
                copy.start()
            for copy in copies:
                copy.wait()
            ffn_kernel(x_ref, *targets, out_ref, active_v)


def stream_and_run(x_ref, sources, targets, out_ref, active_v, gate_sum, up_sum, down_sum, sems):
    copies = load_copies(sources, targets, sems)
    for copy in copies:
        copy.start()
    streamed_ffn(x_ref, targets, out_ref, active_v, gate_sum, up_sum, down_sum, copies)


def ffn_cost(flat, hidden):
    rows, width = flat.shape
    return pl.CostEstimate(
        flops=6 * rows * width * hidden,
        bytes_accessed=6 * width * hidden + 4 * rows * width,
        transcendentals=rows * hidden,
    )


def load_ffn(kernel, section_table, received, present, sources, anywhere, extra=0):
    experts, rows, width = received.shape
    hidden = present[0].shape[1]
    flat = received.reshape(experts * rows, width)
    sums = pltpu.VMEM((flat.shape[0], hidden), jnp.float32)
    produced, *weights = pl.pallas_call(
        kernel,
        out_shape=(
            pltpu.VMEM(flat.shape, jnp.bfloat16),
            *[pltpu.VMEM(w.shape, w.dtype) for w in present] * (1 + extra),
        ),
        in_specs=[spec(pltpu.SMEM)] + [spec(pltpu.VMEM)] * 4 + [spec(pl.ANY if anywhere else pltpu.HBM)] * 3,
        out_specs=(spec(pltpu.VMEM),) * (4 + 3 * extra),
        scratch_shapes=[
            pltpu.VMEM((flat.shape[0], hidden), jnp.bfloat16),
            sums,
            sums,
            pltpu.VMEM(flat.shape, jnp.float32),
            pltpu.SemaphoreType.DMA((2 * (width // K_CUT) + DOWN_PARTS,)),
        ],
        input_output_aliases={2: 1, 3: 2, 4: 3},
        compiler_params=SMALL,
        cost_estimate=ffn_cost(flat, hidden),
        name="load_expert_ffn",
    )(
        section_table,
        in_vmem(flat),
        *[in_vmem(w) for w in present],
        *(sources if anywhere else [in_hbm(w) for w in sources]),
    )
    return produced.reshape(received.shape), weights


def ffn_kernel(x_ref, gate_ref, up_ref, down_ref, out_ref, active_v):
    for c in range(gate_ref.shape[1] // H_CUT):
        cut = pl.ds(c * H_CUT, H_CUT)
        gate_part = jnp.dot(x_ref[...], gate_ref[:, cut], preferred_element_type=jnp.float32)
        up_part = jnp.dot(x_ref[...], up_ref[:, cut], preferred_element_type=jnp.float32)
        active_v[:, cut] = silu_times(gate_part, up_part)
    down_part(active_v, down_ref, out_ref)


def exchange(slots):
    return lax.all_to_all(slots, "expert", 0, 0, tiled=True)


def relay_pairs(step, stages):
    place = list(range(stages))
    for x in range(step % 2, stages - 1, 2):
        place[x], place[x + 1] = x + 1, x
    return [(2 * x + c, 2 * place[x] + c) for x in range(stages) for c in range(2)]


def shards(activations, norm_gain, w_gate, w_up, w_down, routes, gate_scores):
    sections = lax.axis_size("pipe")
    experts = lax.axis_size("expert")
    section = lax.axis_index("pipe")
    stages = sections // 2
    blocks, topk = routes.shape[2:]
    rows = activations.shape[1] // blocks
    lane = rows // 2
    width = activations.shape[2]
    held = (blocks, lane, width)
    slots = (experts, lane, width)
    swap = [(i, i ^ 1) for i in range(sections)]

    def swapped(x):
        return lax.ppermute(x, "pipe", swap)

    route = routes[0, 0].T
    score = gate_scores[0, 0].T
    route_x, gain_x, score_x = swapped(route), swapped(norm_gain), swapped(score)
    own = (w_gate[0, 0], w_up[0, 0], w_down[0, 0])
    *own, route_x, gain_x, score_x = lax.optimization_barrier((*own, route_x, gain_x, score_x))
    other = tuple(swapped(w) for w in own)
    section_table = section.astype(jnp.int32).reshape(1)

    whole_x = activations[0].reshape(blocks, 2, lane, width)
    hidden, sent, gains, *weights_a, ids, scores = first_call(
        held, slots, section_table, route, route_x, score, score_x, whole_x, norm_gain, gain_x, own
    )
    out_a, out_b = [], []
    for step in range(stages):
        received = exchange(sent)
        if step == 0:
            made, weights = load_ffn(first_ffn_kernel, section_table, received, weights_a, other, True, 1)
            weights_a, weights_b = weights[:3], weights[3:]
        else:
            kernel = functools.partial(second_ffn_kernel, CORE_1[step][0])
            made, weights_a = load_ffn(kernel, section_table, received, weights_a, other, True)
        hidden, sent = small_call(
            between_kernel, "mix_norm_pack", (held, slots), (held,), (ids, scores), (hidden, exchange(made), gains)
        )
        out_a.append(hidden)
        received = exchange(sent)
        kernel = functools.partial(second_ffn_kernel, CORE_1[step][1])
        made, weights_b = load_ffn(kernel, section_table, received, weights_b, own, False)
        back = exchange(made)
        if step == stages - 1:
            break
        hidden = small_call(leave_kernel, "mix", (held,), (), (ids, scores), (hidden, back))
        out_b.append(hidden)
        hidden = lax.ppermute(hidden, "pipe", relay_pairs(step, stages))
        sent = small_call(enter_kernel, "norm_pack", (slots,), (held,), (ids,), (hidden, gains))

    kept, leaving = finish(section_table, ids, scores, hidden, back, out_a + out_b)
    whole = join(section_table, kept, swapped(leaving))
    return whole.reshape(1, 1, blocks * rows, width)


def solution(mesh):
    in_specs = (
        P(None, "expert", None),
        P("pipe", None),
        P("pipe", "expert", None, None),
        P("pipe", "expert", None, None),
        P("pipe", "expert", None, None),
        P("pipe", None, "expert", None),
        P("pipe", None, "expert", None),
    )
    out_specs = P("pipe", None, "expert", None)
    return jax.shard_map(shards, mesh=mesh, in_specs=in_specs, out_specs=out_specs, check_vma=False)
```

```python
import jax
import jax.numpy as jnp
from jax import lax
from jax.experimental import pallas as pl
from jax.experimental.pallas import tpu as pltpu
from jax.sharding import PartitionSpec as P

H_CUT = 256
D_CUT = 512
AHEAD = 3
STREAMED = (0,)
K_CUT = 512
DOWN_PARTS = 3
SMALL = pltpu.CompilerParams(vmem_limit_bytes=8 * 1024 * 1024)


def in_vmem(x):
    return pltpu.with_memory_space_constraint(x, pltpu.VMEM)


def in_hbm(x):
    return pltpu.with_memory_space_constraint(x, pltpu.HBM)


def spec(space):
    return pl.BlockSpec(memory_space=space)


def core_of(section_ref):
    return section_ref[0] & 1


def normalised(hidden, gain_row):
    scaled = lax.rsqrt(jnp.mean(hidden * hidden, axis=-1, keepdims=True) + 1e-06)
    return (hidden * scaled * gain_row).astype(jnp.bfloat16)


def mixed(which, ids_ref, scores_ref, hidden_ref, returned_ref, block):
    topk = ids_ref.shape[1]
    parts = [scores_ref[which, k, block] for k in range(topk)]
    whole = parts[0]
    for k in range(1, topk):
        whole = whole + parts[k]
    total = None
    for k in range(topk):
        weight = jnp.full((1, 1), parts[k], jnp.float32) / jnp.full((1, 1), whole, jnp.float32)
        term = returned_ref[ids_ref[which, k, block]].astype(jnp.float32) * weight
        total = term if total is None else total + term
    return (hidden_ref[block].astype(jnp.float32) + total).astype(jnp.bfloat16)


def pack(ids, normed_ref, packed_ref):
    for expert in range(packed_ref.shape[0]):
        block = jnp.int32(0)
        for b in range(1, len(ids)):
            for one in ids[b]:
                block = jnp.where(one == expert, jnp.int32(b), block)
        packed_ref[expert] = normed_ref[block]


def table_ids(which, ids_ref):
    topk, blocks = ids_ref.shape[1:]
    return [[ids_ref[which, k, b] for k in range(topk)] for b in range(blocks)]


def first_kernel(
    section_ref, rx_h, sx_h, gx, ro_h, so_h, go, x_hbm, gate, up, down,
    hidden_ref, packed_ref, gains_ref, gate_v, up_v, down_v, ids_ref, scores_ref,
    ro, rx, so, sx, normed_ref, gain_v, sems, weight_sems,
):
    core = core_of(section_ref)
    first = core == 0
    pairs = (
        (ro_h, ro), (rx_h, rx), (so_h, so), (sx_h, sx),
        (go, gain_v.at[0]), (gx, gain_v.at[1]), (x_hbm.at[:, core], hidden_ref),
    )
    copies = [pltpu.make_async_copy(source, target, sems.at[i]) for i, (source, target) in enumerate(pairs)]
    for copy in copies:
        copy.start()
    for copy in copies:
        copy.wait()
    loads = [
        pltpu.make_async_copy(source, target, weight_sems.at[i])
        for i, (source, target) in enumerate(((gate, gate_v), (up, up_v), (down, down_v)))
    ]

    topk, blocks = ro.shape
    ids = [[None] * topk for _ in range(blocks)]
    for b in range(blocks):
        for k in range(topk):
            ids[b][k] = jnp.where(first, ro[k, b], rx[k, b])
            ids_ref[0, k, b] = ids[b][k]
            ids_ref[1, k, b] = jnp.where(first, rx[k, b], ro[k, b])
            scores_ref[0, k, b] = jnp.where(first, so[k, b], sx[k, b])
            scores_ref[1, k, b] = jnp.where(first, sx[k, b], so[k, b])
    own = gain_v[0].astype(jnp.float32)
    other = gain_v[1].astype(jnp.float32)
    gain = jnp.where(first, own, other)
    gains_ref[0] = gain
    gains_ref[1] = jnp.where(first, other, own)
    for block in range(hidden_ref.shape[0]):
        normed_ref[block] = normalised(hidden_ref[block].astype(jnp.float32), gain)
    pack(ids, normed_ref, packed_ref)

    @pl.when(first)
    def _():
        for copy in loads:
            copy.start()
        for copy in loads:
            copy.wait()


def first_call(held, slots, section_table, route, route_x, score, score_x, whole_x, gain, gain_x, own):
    width = held[2]
    both = (2,) + route.shape
    return pl.pallas_call(
        first_kernel,
        out_shape=(
            pltpu.VMEM(held, jnp.bfloat16),
            pltpu.VMEM(slots, jnp.bfloat16),
            pltpu.VMEM((2, 1, width), jnp.float32),
            *[pltpu.VMEM(w.shape, w.dtype) for w in own],
            pltpu.SMEM(both, jnp.int32),
            pltpu.SMEM(both, jnp.float32),
        ),
        in_specs=[spec(pltpu.SMEM)] + [spec(pl.ANY)] * 3 + [spec(pltpu.HBM)] * 7,
        out_specs=(spec(pltpu.VMEM),) * 6 + (spec(pltpu.SMEM),) * 2,
        scratch_shapes=[
            pltpu.SMEM(route.shape, jnp.int32),
            pltpu.SMEM(route.shape, jnp.int32),
            pltpu.SMEM(route.shape, jnp.float32),
            pltpu.SMEM(route.shape, jnp.float32),
            pltpu.VMEM(held, jnp.bfloat16),
            pltpu.VMEM((2, 1, width), jnp.bfloat16),
            pltpu.SemaphoreType.DMA((7,)),
            pltpu.SemaphoreType.DMA((3,)),
        ],
        compiler_params=SMALL,
        name="slice_norm_pack",
    )(section_table, route_x, score_x, gain_x, *[in_hbm(v) for v in (route, score, gain, whole_x, *own)])


def enter_kernel(ids_ref, hidden_ref, gains_ref, packed_ref, normed_ref):
    for block in range(hidden_ref.shape[0]):
        normed_ref[block] = normalised(hidden_ref[block].astype(jnp.float32), gains_ref[0])
    pack(table_ids(0, ids_ref), normed_ref, packed_ref)


def between_kernel(ids_ref, scores_ref, hidden_ref, returned_ref, gains_ref, out_ref, packed_ref, normed_ref):
    for block in range(hidden_ref.shape[0]):
        result = mixed(0, ids_ref, scores_ref, hidden_ref, returned_ref, block)
        out_ref[block] = result
        normed_ref[block] = normalised(result.astype(jnp.float32), gains_ref[1])
    pack(table_ids(1, ids_ref), normed_ref, packed_ref)


def leave_kernel(ids_ref, scores_ref, hidden_ref, returned_ref, out_ref):
    for block in range(hidden_ref.shape[0]):
        out_ref[block] = mixed(1, ids_ref, scores_ref, hidden_ref, returned_ref, block)


def finish_kernel(section_ref, ids_ref, scores_ref, hidden_ref, returned_ref, *refs):
    earlier, (kept_ref, sent_ref, last_ref, sems) = refs[:-4], refs[-4:]
    stages = (len(earlier) + 1) // 2
    for block in range(hidden_ref.shape[0]):
        last_ref[block] = mixed(1, ids_ref, scores_ref, hidden_ref, returned_ref, block)
    results_a, results_b = earlier[:stages], (*earlier[stages:], last_ref)
    for step in range(stages):
        for core, targets in ((0, (kept_ref, sent_ref)), (1, (sent_ref, kept_ref))):

            @pl.when(section_ref[0] == 2 * step + core)
            def _():
                for i, source in enumerate((results_a[step], results_b[step])):
                    pltpu.make_async_copy(source, targets[i], sems.at[i]).start()

    for i, target in enumerate((kept_ref, sent_ref)):
        pltpu.make_async_copy(results_a[0], target, sems.at[i]).wait()


def finish(section_table, ids, scores, hidden, returned, earlier):
    held = hidden.shape
    return pl.pallas_call(
        finish_kernel,
        out_shape=(pltpu.VMEM(held, jnp.bfloat16),) * 2,
        in_specs=[spec(pltpu.SMEM)] * 3 + [spec(pltpu.VMEM)] * 2 + [spec(pl.ANY)] * len(earlier),
        out_specs=(spec(pltpu.VMEM),) * 2,
        scratch_shapes=[pltpu.VMEM(held, jnp.bfloat16), pltpu.SemaphoreType.DMA((2,))],
        compiler_params=SMALL,
        name="mix_choose",
    )(section_table, ids, scores, in_vmem(hidden), in_vmem(returned), *earlier)


def join_kernel(section_ref, kept_ref, got_ref, out_ref, sems):
    copies = [
        pltpu.make_async_copy(kept_ref, out_ref.at[:, core_of(section_ref)], sems.at[0]),
        pltpu.make_async_copy(got_ref, out_ref.at[:, 1 - core_of(section_ref)], sems.at[1]),
    ]
    for copy in copies:
        copy.start()
    for copy in copies:
        copy.wait()


def join(section_table, kept, got):
    blocks, lane, width = kept.shape
    return pl.pallas_call(
        join_kernel,
        out_shape=pltpu.HBM((blocks, 2, lane, width), jnp.bfloat16),
        in_specs=[spec(pltpu.SMEM)] + [spec(pltpu.VMEM)] * 2,
        out_specs=spec(pltpu.HBM),
        scratch_shapes=[pltpu.SemaphoreType.DMA((2,))],
        compiler_params=SMALL,
        name="join_rows",
    )(section_table, in_vmem(kept), in_vmem(got))


def small_call(kernel, name, outs, scratch, smem, vmem):
    single = len(outs) == 1
    shapes = tuple(pltpu.VMEM(o, jnp.bfloat16) for o in outs)
    specs = tuple(spec(pltpu.VMEM) for _ in outs)
    return pl.pallas_call(
        kernel,
        out_shape=shapes[0] if single else shapes,
        in_specs=[spec(pltpu.SMEM)] * len(smem) + [spec(pltpu.VMEM)] * len(vmem),
        out_specs=specs[0] if single else specs,
        scratch_shapes=[pltpu.VMEM(s, jnp.bfloat16) for s in scratch],
        compiler_params=SMALL,
        name=name,
    )(*smem, *[in_vmem(v) for v in vmem])


def silu_times(gate_part, up_part):
    return (gate_part / (1.0 + jnp.exp(-gate_part)) * up_part).astype(jnp.bfloat16)


def down_part(active_v, down_ref, out_ref):
    for c in range(down_ref.shape[1] // D_CUT):
        cut = pl.ds(c * D_CUT, D_CUT)
        produced = jnp.dot(active_v[...], down_ref[:, cut], preferred_element_type=jnp.float32)
        out_ref[:, cut] = produced.astype(jnp.bfloat16)


def load_copies(sources, targets, sems):
    (gate, up, down), (gate_ref, up_ref, down_ref) = sources, targets
    parts = gate_ref.shape[0] // K_CUT
    down_rows = down_ref.shape[0] // DOWN_PARTS
    made = []
    for c in range(parts):
        cut = pl.ds(c * K_CUT, K_CUT)
        made.append(pltpu.make_async_copy(gate.at[cut], gate_ref.at[cut], sems.at[2 * c]))
        made.append(pltpu.make_async_copy(up.at[cut], up_ref.at[cut], sems.at[2 * c + 1]))
    for c in range(DOWN_PARTS):
        cut = pl.ds(c * down_rows, down_rows)
        made.append(pltpu.make_async_copy(down.at[cut], down_ref.at[cut], sems.at[2 * parts + c]))
    return made


def streamed_ffn(x_ref, targets, out_ref, active_v, gate_sum, up_sum, down_sum, ready):
    gate_ref, up_ref, down_ref = targets
    parts = gate_ref.shape[0] // K_CUT
    for c in range(parts):
        cut = pl.ds(c * K_CUT, K_CUT)
        for i, weight_ref, sum_ref in ((2 * c, gate_ref, gate_sum), (2 * c + 1, up_ref, up_sum)):
            ready(i)
            term = jnp.dot(x_ref[:, cut], weight_ref[cut, :], preferred_element_type=jnp.float32)
            sum_ref[...] = term if c == 0 else sum_ref[...] + term
    active_v[...] = silu_times(gate_sum[...], up_sum[...])
    down_rows = down_ref.shape[0] // DOWN_PARTS
    for c in range(DOWN_PARTS):
        ready(2 * parts + c)
        cut = pl.ds(c * down_rows, down_rows)
        term = jnp.dot(active_v[:, cut], down_ref[cut, :], preferred_element_type=jnp.float32)
        if c == 0:
            down_sum[...] = term
        elif c < DOWN_PARTS - 1:
            down_sum[...] += term
        else:
            out_ref[...] = (down_sum[...] + term).astype(jnp.bfloat16)


def stream_on_core_1(section_ref, copies):
    def start():
        @pl.when(core_of(section_ref) != 0)
        def _():
            for copy in copies:
                copy.start()

    def ready(i):
        @pl.when(core_of(section_ref) != 0)
        def _():
            copies[i].wait()

    return start, ready


def first_ffn_kernel(
    section_ref, x_ref, gi, ui, di, gx, ux, dx, out_ref, gate_ref, up_ref, down_ref, gate_next, up_next, down_next,
    active_v, gate_sum, up_sum, down_sum, sems
):
    targets = (gate_ref, up_ref, down_ref)
    start, ready = stream_on_core_1(section_ref, load_copies((gx, ux, dx), targets, sems))
    copies = load_copies((gx, ux, dx), (gate_next, up_next, down_next), sems)
    start()

    @pl.when(core_of(section_ref) == 0)
    def _():
        for copy in copies:
            copy.start()
        for copy in copies[:AHEAD]:
            copy.wait()

    streamed_ffn(x_ref, targets, out_ref, active_v, gate_sum, up_sum, down_sum, ready)

    @pl.when(core_of(section_ref) == 0)
    def _():
        for copy in copies[AHEAD:]:
            copy.wait()


def second_ffn_kernel(
    section_ref, x_ref, gi, ui, di, g_h, u_h, d_h, out_ref, gate_ref, up_ref, down_ref,
    active_v, gate_sum, up_sum, down_sum, sems
):
    targets = (gate_ref, up_ref, down_ref)
    start, ready = stream_on_core_1(section_ref, load_copies((g_h, u_h, d_h), targets, sems))
    start()
    streamed_ffn(x_ref, targets, out_ref, active_v, gate_sum, up_sum, down_sum, ready)


def later_ffn_kernel(
    section_ref, x_ref, gi, ui, di, g_h, u_h, d_h, out_ref, gate_ref, up_ref, down_ref,
    active_v, gate_sum, up_sum, down_sum, sems
):
    @pl.when(core_of(section_ref) != 0)
    def _():
        copies = load_copies((g_h, u_h, d_h), (gate_ref, up_ref, down_ref), sems)
        for copy in copies:
            copy.start()
        for copy in copies:
            copy.wait()

    ffn_kernel(x_ref, gate_ref, up_ref, down_ref, out_ref, active_v)


def ffn_cost(flat, hidden):
    rows, width = flat.shape
    return pl.CostEstimate(
        flops=6 * rows * width * hidden,
        bytes_accessed=6 * width * hidden + 4 * rows * width,
        transcendentals=rows * hidden,
    )


def load_ffn(kernel, section_table, received, present, sources, anywhere, extra=0):
    experts, rows, width = received.shape
    hidden = present[0].shape[1]
    flat = received.reshape(experts * rows, width)
    sums = pltpu.VMEM((flat.shape[0], hidden), jnp.float32)
    produced, *weights = pl.pallas_call(
        kernel,
        out_shape=(
            pltpu.VMEM(flat.shape, jnp.bfloat16),
            *[pltpu.VMEM(w.shape, w.dtype) for w in present] * (1 + extra),
        ),
        in_specs=[spec(pltpu.SMEM)] + [spec(pltpu.VMEM)] * 4 + [spec(pl.ANY if anywhere else pltpu.HBM)] * 3,
        out_specs=(spec(pltpu.VMEM),) * (4 + 3 * extra),
        scratch_shapes=[
            pltpu.VMEM((flat.shape[0], hidden), jnp.bfloat16),
            sums,
            sums,
            pltpu.VMEM(flat.shape, jnp.float32),
            pltpu.SemaphoreType.DMA((2 * (width // K_CUT) + DOWN_PARTS,)),
        ],
        input_output_aliases={2: 1, 3: 2, 4: 3},
        compiler_params=SMALL,
        cost_estimate=ffn_cost(flat, hidden),
        name="load_expert_ffn",
    )(
        section_table,
        in_vmem(flat),
        *[in_vmem(w) for w in present],
        *(sources if anywhere else [in_hbm(w) for w in sources]),
    )
    return produced.reshape(received.shape), weights


def ffn_kernel(x_ref, gate_ref, up_ref, down_ref, out_ref, active_v):
    for c in range(gate_ref.shape[1] // H_CUT):
        cut = pl.ds(c * H_CUT, H_CUT)
        gate_part = jnp.dot(x_ref[...], gate_ref[:, cut], preferred_element_type=jnp.float32)
        up_part = jnp.dot(x_ref[...], up_ref[:, cut], preferred_element_type=jnp.float32)
        active_v[:, cut] = silu_times(gate_part, up_part)
    down_part(active_v, down_ref, out_ref)


def exchange(slots):
    return lax.all_to_all(slots, "expert", 0, 0, tiled=True)


def relay_pairs(step, stages):
    place = list(range(stages))
    for x in range(step % 2, stages - 1, 2):
        place[x], place[x + 1] = x + 1, x
    return [(2 * x + c, 2 * place[x] + c) for x in range(stages) for c in range(2)]


def shards(activations, norm_gain, w_gate, w_up, w_down, routes, gate_scores):
    sections = lax.axis_size("pipe")
    experts = lax.axis_size("expert")
    section = lax.axis_index("pipe")
    stages = sections // 2
    blocks, topk = routes.shape[2:]
    rows = activations.shape[1] // blocks
    lane = rows // 2
    width = activations.shape[2]
    held = (blocks, lane, width)
    slots = (experts, lane, width)
    swap = [(i, i ^ 1) for i in range(sections)]

    def swapped(x):
        return lax.ppermute(x, "pipe", swap)

    route = routes[0, 0].T
    score = gate_scores[0, 0].T
    route_x, gain_x, score_x = swapped(route), swapped(norm_gain), swapped(score)
    own = (w_gate[0, 0], w_up[0, 0], w_down[0, 0])
    *own, route_x, gain_x, score_x = lax.optimization_barrier((*own, route_x, gain_x, score_x))
    other = tuple(swapped(w) for w in own)
    section_table = section.astype(jnp.int32).reshape(1)

    whole_x = activations[0].reshape(blocks, 2, lane, width)
    hidden, sent, gains, *weights_a, ids, scores = first_call(
        held, slots, section_table, route, route_x, score, score_x, whole_x, norm_gain, gain_x, own
    )
    out_a, out_b = [], []
    for step in range(stages):
        received = exchange(sent)
        if step == 0:
            made, weights = load_ffn(first_ffn_kernel, section_table, received, weights_a, other, True, 1)
            weights_a, weights_b = weights[:3], weights[3:]
        else:
            made, weights_a = load_ffn(later_ffn_kernel, section_table, received, weights_a, other, True)
        hidden, sent = small_call(
            between_kernel, "mix_norm_pack", (held, slots), (held,), (ids, scores), (hidden, exchange(made), gains)
        )
        out_a.append(hidden)
        received = exchange(sent)
        kernel = second_ffn_kernel if step in STREAMED else later_ffn_kernel
        made, weights_b = load_ffn(kernel, section_table, received, weights_b, own, False)
        back = exchange(made)
        if step == stages - 1:
            break
        hidden = small_call(leave_kernel, "mix", (held,), (), (ids, scores), (hidden, back))
        out_b.append(hidden)
        hidden = lax.ppermute(hidden, "pipe", relay_pairs(step, stages))
        sent = small_call(enter_kernel, "norm_pack", (slots,), (held,), (ids,), (hidden, gains))

    kept, leaving = finish(section_table, ids, scores, hidden, back, out_a + out_b)
    whole = join(section_table, kept, swapped(leaving))
    return whole.reshape(1, 1, blocks * rows, width)


def solution(mesh):
    in_specs = (
        P(None, "expert", None),
        P("pipe", None),
        P("pipe", "expert", None, None),
        P("pipe", "expert", None, None),
        P("pipe", "expert", None, None),
        P("pipe", None, "expert", None),
        P("pipe", None, "expert", None),
    )
    out_specs = P("pipe", None, "expert", None)
    return jax.shard_map(shards, mesh=mesh, in_specs=in_specs, out_specs=out_specs, check_vma=False)
```

```python
import functools

import jax
import jax.numpy as jnp
from jax import lax
from jax.experimental import pallas as pl
from jax.experimental.pallas import tpu as pltpu
from jax.sharding import PartitionSpec as P

H_CUT = 256
D_CUT = 512
AHEAD = 8
KEPT = (1,)
K_CUT = 512
DOWN_PARTS = 3
SMALL = pltpu.CompilerParams(vmem_limit_bytes=8 * 1024 * 1024)


def in_vmem(x):
    return pltpu.with_memory_space_constraint(x, pltpu.VMEM)


def in_hbm(x):
    return pltpu.with_memory_space_constraint(x, pltpu.HBM)


def spec(space):
    return pl.BlockSpec(memory_space=space)


def core_of(section_ref):
    return section_ref[0] & 1


def working(section_ref, step):
    return (section_ref[0] >> 1) == step


def normalised(hidden, gain_row):
    scaled = lax.rsqrt(jnp.mean(hidden * hidden, axis=-1, keepdims=True) + 1e-06)
    return (hidden * scaled * gain_row).astype(jnp.bfloat16)


def mixed(which, ids_ref, scores_ref, hidden_ref, returned_ref, block):
    topk = ids_ref.shape[1]
    parts = [scores_ref[which, k, block] for k in range(topk)]
    whole = parts[0]
    for k in range(1, topk):
        whole = whole + parts[k]
    total = None
    for k in range(topk):
        weight = jnp.full((1, 1), parts[k], jnp.float32) / jnp.full((1, 1), whole, jnp.float32)
        term = returned_ref[ids_ref[which, k, block]].astype(jnp.float32) * weight
        total = term if total is None else total + term
    return (hidden_ref[block].astype(jnp.float32) + total).astype(jnp.bfloat16)


def pack(ids, normed_ref, packed_ref):
    for expert in range(packed_ref.shape[0]):
        block = jnp.int32(0)
        for b in range(1, len(ids)):
            for one in ids[b]:
                block = jnp.where(one == expert, jnp.int32(b), block)
        packed_ref[expert] = normed_ref[block]


def table_ids(which, ids_ref):
    topk, blocks = ids_ref.shape[1:]
    return [[ids_ref[which, k, b] for k in range(topk)] for b in range(blocks)]


def first_kernel(
    section_ref, rx_h, sx_h, gx, ro_h, so_h, go, x_hbm, gate, up, down,
    hidden_ref, packed_ref, gains_ref, gate_v, up_v, down_v, ids_ref, scores_ref,
    ro, rx, so, sx, normed_ref, gain_v, sems, weight_sems,
):
    core = core_of(section_ref)
    first = core == 0
    pairs = (
        (ro_h, ro), (rx_h, rx), (so_h, so), (sx_h, sx),
        (go, gain_v.at[0]), (gx, gain_v.at[1]), (x_hbm.at[:, core], hidden_ref),
    )
    copies = [pltpu.make_async_copy(source, target, sems.at[i]) for i, (source, target) in enumerate(pairs)]
    for copy in copies:
        copy.start()
    for copy in copies:
        copy.wait()
    loads = [
        pltpu.make_async_copy(source, target, weight_sems.at[i])
        for i, (source, target) in enumerate(((gate, gate_v), (up, up_v), (down, down_v)))
    ]

    topk, blocks = ro.shape
    ids = [[None] * topk for _ in range(blocks)]
    for b in range(blocks):
        for k in range(topk):
            ids[b][k] = jnp.where(first, ro[k, b], rx[k, b])
            ids_ref[0, k, b] = ids[b][k]
            ids_ref[1, k, b] = jnp.where(first, rx[k, b], ro[k, b])
            scores_ref[0, k, b] = jnp.where(first, so[k, b], sx[k, b])
            scores_ref[1, k, b] = jnp.where(first, sx[k, b], so[k, b])
    own = gain_v[0].astype(jnp.float32)
    other = gain_v[1].astype(jnp.float32)
    gain = jnp.where(first, own, other)
    gains_ref[0] = gain
    gains_ref[1] = jnp.where(first, other, own)
    for block in range(hidden_ref.shape[0]):
        normed_ref[block] = normalised(hidden_ref[block].astype(jnp.float32), gain)
    pack(ids, normed_ref, packed_ref)

    @pl.when(first)
    def _():
        for copy in loads:
            copy.start()
        for copy in loads:
            copy.wait()


def first_call(held, slots, section_table, route, route_x, score, score_x, whole_x, gain, gain_x, own):
    width = held[2]
    both = (2,) + route.shape
    return pl.pallas_call(
        first_kernel,
        out_shape=(
            pltpu.VMEM(held, jnp.bfloat16),
            pltpu.VMEM(slots, jnp.bfloat16),
            pltpu.VMEM((2, 1, width), jnp.float32),
            *[pltpu.VMEM(w.shape, w.dtype) for w in own],
            pltpu.SMEM(both, jnp.int32),
            pltpu.SMEM(both, jnp.float32),
        ),
        in_specs=[spec(pltpu.SMEM)] + [spec(pl.ANY)] * 3 + [spec(pltpu.HBM)] * 7,
        out_specs=(spec(pltpu.VMEM),) * 6 + (spec(pltpu.SMEM),) * 2,
        scratch_shapes=[
            pltpu.SMEM(route.shape, jnp.int32),
            pltpu.SMEM(route.shape, jnp.int32),
            pltpu.SMEM(route.shape, jnp.float32),
            pltpu.SMEM(route.shape, jnp.float32),
            pltpu.VMEM(held, jnp.bfloat16),
            pltpu.VMEM((2, 1, width), jnp.bfloat16),
            pltpu.SemaphoreType.DMA((7,)),
            pltpu.SemaphoreType.DMA((3,)),
        ],
        compiler_params=SMALL,
        name="slice_norm_pack",
    )(section_table, route_x, score_x, gain_x, *[in_hbm(v) for v in (route, score, gain, whole_x, *own)])


def enter_kernel(ids_ref, hidden_ref, gains_ref, packed_ref, normed_ref):
    for block in range(hidden_ref.shape[0]):
        normed_ref[block] = normalised(hidden_ref[block].astype(jnp.float32), gains_ref[0])
    pack(table_ids(0, ids_ref), normed_ref, packed_ref)


def between_kernel(ids_ref, scores_ref, hidden_ref, returned_ref, gains_ref, out_ref, packed_ref, normed_ref):
    for block in range(hidden_ref.shape[0]):
        result = mixed(0, ids_ref, scores_ref, hidden_ref, returned_ref, block)
        out_ref[block] = result
        normed_ref[block] = normalised(result.astype(jnp.float32), gains_ref[1])
    pack(table_ids(1, ids_ref), normed_ref, packed_ref)


def leave_kernel(ids_ref, scores_ref, hidden_ref, returned_ref, out_ref):
    for block in range(hidden_ref.shape[0]):
        out_ref[block] = mixed(1, ids_ref, scores_ref, hidden_ref, returned_ref, block)


def finish_kernel(section_ref, ids_ref, scores_ref, hidden_ref, returned_ref, *refs):
    earlier, (kept_ref, sent_ref, last_ref, sems) = refs[:-4], refs[-4:]
    stages = (len(earlier) + 1) // 2
    for block in range(hidden_ref.shape[0]):
        last_ref[block] = mixed(1, ids_ref, scores_ref, hidden_ref, returned_ref, block)
    results_a, results_b = earlier[:stages], (*earlier[stages:], last_ref)
    for step in range(stages):
        for core, targets in ((0, (kept_ref, sent_ref)), (1, (sent_ref, kept_ref))):

            @pl.when(section_ref[0] == 2 * step + core)
            def _():
                for i, source in enumerate((results_a[step], results_b[step])):
                    pltpu.make_async_copy(source, targets[i], sems.at[i]).start()

    for i, target in enumerate((kept_ref, sent_ref)):
        pltpu.make_async_copy(results_a[0], target, sems.at[i]).wait()


def finish(section_table, ids, scores, hidden, returned, earlier):
    held = hidden.shape
    return pl.pallas_call(
        finish_kernel,
        out_shape=(pltpu.VMEM(held, jnp.bfloat16),) * 2,
        in_specs=[spec(pltpu.SMEM)] * 3 + [spec(pltpu.VMEM)] * 2 + [spec(pl.ANY)] * len(earlier),
        out_specs=(spec(pltpu.VMEM),) * 2,
        scratch_shapes=[pltpu.VMEM(held, jnp.bfloat16), pltpu.SemaphoreType.DMA((2,))],
        compiler_params=SMALL,
        name="mix_choose",
    )(section_table, ids, scores, in_vmem(hidden), in_vmem(returned), *earlier)


def join_kernel(section_ref, kept_ref, got_ref, out_ref, sems):
    lane = core_of(section_ref)
    copies = [
        pltpu.make_async_copy(kept_ref, out_ref.at[:, lane], sems.at[0]),
        pltpu.make_async_copy(got_ref, out_ref.at[:, 1 - lane], sems.at[1]),
    ]
    for copy in copies:
        copy.start()
    for copy in copies:
        copy.wait()


def join(section_table, kept, got):
    blocks, lane, width = kept.shape
    return pl.pallas_call(
        join_kernel,
        out_shape=pltpu.HBM((blocks, 2, lane, width), jnp.bfloat16),
        in_specs=[spec(pltpu.SMEM)] + [spec(pltpu.VMEM)] * 2,
        out_specs=spec(pltpu.HBM),
        scratch_shapes=[pltpu.SemaphoreType.DMA((2,))],
        compiler_params=SMALL,
        name="join_rows",
    )(section_table, in_vmem(kept), in_vmem(got))


def small_call(kernel, name, outs, scratch, smem, vmem):
    single = len(outs) == 1
    shapes = tuple(pltpu.VMEM(o, jnp.bfloat16) for o in outs)
    specs = tuple(spec(pltpu.VMEM) for _ in outs)
    return pl.pallas_call(
        kernel,
        out_shape=shapes[0] if single else shapes,
        in_specs=[spec(pltpu.SMEM)] * len(smem) + [spec(pltpu.VMEM)] * len(vmem),
        out_specs=specs[0] if single else specs,
        scratch_shapes=[pltpu.VMEM(s, jnp.bfloat16) for s in scratch],
        compiler_params=SMALL,
        name=name,
    )(*smem, *[in_vmem(v) for v in vmem])


def silu_times(gate_part, up_part):
    return (gate_part / (1.0 + jnp.exp(-gate_part)) * up_part).astype(jnp.bfloat16)


def down_part(active_v, down_ref, out_ref):
    for c in range(down_ref.shape[1] // D_CUT):
        cut = pl.ds(c * D_CUT, D_CUT)
        produced = jnp.dot(active_v[...], down_ref[:, cut], preferred_element_type=jnp.float32)
        out_ref[:, cut] = produced.astype(jnp.bfloat16)


def load_copies(sources, targets, sems):
    (gate, up, down), (gate_ref, up_ref, down_ref) = sources, targets
    parts = gate_ref.shape[0] // K_CUT
    down_rows = down_ref.shape[0] // DOWN_PARTS
    made = []
    for c in range(parts):
        cut = pl.ds(c * K_CUT, K_CUT)
        made.append(pltpu.make_async_copy(gate.at[cut], gate_ref.at[cut], sems.at[2 * c]))
        made.append(pltpu.make_async_copy(up.at[cut], up_ref.at[cut], sems.at[2 * c + 1]))
    for c in range(DOWN_PARTS):
        cut = pl.ds(c * down_rows, down_rows)
        made.append(pltpu.make_async_copy(down.at[cut], down_ref.at[cut], sems.at[2 * parts + c]))
    return made


def streamed_ffn(x_ref, targets, out_ref, active_v, gate_sum, up_sum, down_sum, ready):
    gate_ref, up_ref, down_ref = targets
    parts = gate_ref.shape[0] // K_CUT
    for c in range(parts):
        cut = pl.ds(c * K_CUT, K_CUT)
        for i, weight_ref, sum_ref in ((2 * c, gate_ref, gate_sum), (2 * c + 1, up_ref, up_sum)):
            ready(i)
            term = jnp.dot(x_ref[:, cut], weight_ref[cut, :], preferred_element_type=jnp.float32)
            sum_ref[...] = term if c == 0 else sum_ref[...] + term
    active_v[...] = silu_times(gate_sum[...], up_sum[...])
    down_rows = down_ref.shape[0] // DOWN_PARTS
    for c in range(DOWN_PARTS):
        ready(2 * parts + c)
        cut = pl.ds(c * down_rows, down_rows)
        term = jnp.dot(active_v[:, cut], down_ref[cut, :], preferred_element_type=jnp.float32)
        if c == 0:
            down_sum[...] = term
        elif c < DOWN_PARTS - 1:
            down_sum[...] += term
        else:
            out_ref[...] = (down_sum[...] + term).astype(jnp.bfloat16)


def first_ffn_kernel(
    section_ref, x_ref, gi, ui, di, gx, ux, dx, out_ref, gate_ref, up_ref, down_ref, gate_next, up_next, down_next,
    active_v, gate_sum, up_sum, down_sum, sems
):
    targets = (gate_ref, up_ref, down_ref)

    @pl.when(core_of(section_ref) == 0)
    def _():
        copies = load_copies((gx, ux, dx), (gate_next, up_next, down_next), sems)
        for copy in copies:
            copy.start()
        for copy in copies[:AHEAD]:
            copy.wait()

        @pl.when(working(section_ref, 0))
        def _():
            ffn_body(x_ref, *targets, out_ref, active_v)

        for copy in copies[AHEAD:]:
            copy.wait()

    @pl.when(core_of(section_ref) != 0)
    def _():
        stream_and_run(section_ref, x_ref, (gx, ux, dx), targets, out_ref, active_v, gate_sum, up_sum, down_sum, sems)


def stream_and_run(section_ref, x_ref, sources, targets, out_ref, active_v, gate_sum, up_sum, down_sum, sems):
    copies = load_copies(sources, targets, sems)
    for copy in copies:
        copy.start()

    @pl.when(working(section_ref, 0))
    def _():
        streamed_ffn(x_ref, targets, out_ref, active_v, gate_sum, up_sum, down_sum, lambda i: copies[i].wait())

    @pl.when(jnp.logical_not(working(section_ref, 0)))
    def _():
        for copy in copies:
            copy.wait()


def second_ffn_kernel(
    section_ref, x_ref, gi, ui, di, g_h, u_h, d_h, out_ref, gate_ref, up_ref, down_ref,
    active_v, gate_sum, up_sum, down_sum, sems
):
    targets = (gate_ref, up_ref, down_ref)

    @pl.when(jnp.logical_and(core_of(section_ref) == 0, working(section_ref, 0)))
    def _():
        ffn_body(x_ref, *targets, out_ref, active_v)

    @pl.when(core_of(section_ref) != 0)
    def _():
        stream_and_run(section_ref, x_ref, (g_h, u_h, d_h), targets, out_ref, active_v, gate_sum, up_sum, down_sum, sems)


def later_ffn_kernel(
    step, section_ref, x_ref, gi, ui, di, g_h, u_h, d_h, out_ref, gate_ref, up_ref, down_ref,
    active_v, gate_sum, up_sum, down_sum, sems
):
    @pl.when(core_of(section_ref) != 0)
    def _():
        copies = load_copies((g_h, u_h, d_h), (gate_ref, up_ref, down_ref), sems)
        for copy in copies:
            copy.start()
        for copy in copies:
            copy.wait()

    @pl.when(working(section_ref, step))
    def _():
        ffn_body(x_ref, gate_ref, up_ref, down_ref, out_ref, active_v)


def ffn_cost(flat, hidden):
    rows, width = flat.shape
    return pl.CostEstimate(
        flops=6 * rows * width * hidden,
        bytes_accessed=6 * width * hidden + 4 * rows * width,
        transcendentals=rows * hidden,
    )


def load_ffn(kernel, section_table, received, present, sources, anywhere, extra=0):
    experts, rows, width = received.shape
    hidden = present[0].shape[1]
    flat = received.reshape(experts * rows, width)
    sums = pltpu.VMEM((flat.shape[0], hidden), jnp.float32)
    produced, *weights = pl.pallas_call(
        kernel,
        out_shape=(
            pltpu.VMEM(flat.shape, jnp.bfloat16),
            *[pltpu.VMEM(w.shape, w.dtype) for w in present] * (1 + extra),
        ),
        in_specs=[spec(pltpu.SMEM)] + [spec(pltpu.VMEM)] * 4 + [spec(pl.ANY if anywhere else pltpu.HBM)] * 3,
        out_specs=(spec(pltpu.VMEM),) * (4 + 3 * extra),
        scratch_shapes=[
            pltpu.VMEM((flat.shape[0], hidden), jnp.bfloat16),
            sums,
            sums,
            pltpu.VMEM(flat.shape, jnp.float32),
            pltpu.SemaphoreType.DMA((2 * (width // K_CUT) + DOWN_PARTS,)),
        ],
        input_output_aliases={2: 1, 3: 2, 4: 3},
        compiler_params=SMALL,
        cost_estimate=ffn_cost(flat, hidden),
        name="load_expert_ffn",
    )(
        section_table,
        in_vmem(flat),
        *[in_vmem(w) for w in present],
        *(sources if anywhere else [in_hbm(w) for w in sources]),
    )
    return produced.reshape(received.shape), weights


def ffn_body(x_ref, gate_ref, up_ref, down_ref, out_ref, active_v):
    for c in range(gate_ref.shape[1] // H_CUT):
        cut = pl.ds(c * H_CUT, H_CUT)
        gate_part = jnp.dot(x_ref[...], gate_ref[:, cut], preferred_element_type=jnp.float32)
        up_part = jnp.dot(x_ref[...], up_ref[:, cut], preferred_element_type=jnp.float32)
        active_v[:, cut] = silu_times(gate_part, up_part)
    down_part(active_v, down_ref, out_ref)


def ffn_kernel(step, section_ref, x_ref, gate_ref, up_ref, down_ref, out_ref, active_v):
    @pl.when(working(section_ref, step))
    def _():
        ffn_body(x_ref, gate_ref, up_ref, down_ref, out_ref, active_v)


def ffn(step, section_table, received, weights):
    experts, rows, width = received.shape
    flat = received.reshape(experts * rows, width)
    hidden = weights[0].shape[1]
    produced = pl.pallas_call(
        functools.partial(ffn_kernel, step),
        out_shape=pltpu.VMEM(flat.shape, jnp.bfloat16),
        in_specs=[spec(pltpu.SMEM)] + [spec(pltpu.VMEM)] * 4,
        out_specs=spec(pltpu.VMEM),
        scratch_shapes=[pltpu.VMEM((flat.shape[0], hidden), jnp.bfloat16)],
        compiler_params=SMALL,
        cost_estimate=ffn_cost(flat, hidden),
        name="expert_ffn",
    )(section_table, in_vmem(flat), *[in_vmem(w) for w in weights])
    return produced.reshape(received.shape)


def exchange(slots):
    return lax.all_to_all(slots, "expert", 0, 0, tiled=True)


def relay_pairs(step, stages):
    place = list(range(stages))
    for x in range(step % 2, stages - 1, 2):
        place[x], place[x + 1] = x + 1, x
    if step % 2:
        place[0], place[-1] = stages - 1, 0
    return [(2 * x + c, 2 * place[x] + c) for x in range(stages) for c in range(2)]


def shards(activations, norm_gain, w_gate, w_up, w_down, routes, gate_scores):
    sections = lax.axis_size("pipe")
    experts = lax.axis_size("expert")
    section = lax.axis_index("pipe")
    stages = sections // 2
    blocks, topk = routes.shape[2:]
    rows = activations.shape[1] // blocks
    lane = rows // 2
    width = activations.shape[2]
    held = (blocks, lane, width)
    slots = (experts, lane, width)
    swap = [(i, i ^ 1) for i in range(sections)]

    def swapped(x):
        return lax.ppermute(x, "pipe", swap)

    route = routes[0, 0].T
    score = gate_scores[0, 0].T
    route_x, gain_x, score_x = swapped(route), swapped(norm_gain), swapped(score)
    own = (w_gate[0, 0], w_up[0, 0], w_down[0, 0])
    *own, route_x, gain_x, score_x = lax.optimization_barrier((*own, route_x, gain_x, score_x))
    other = tuple(swapped(w) for w in own)
    section_table = section.astype(jnp.int32).reshape(1)

    whole_x = activations[0].reshape(blocks, 2, lane, width)
    hidden, sent, gains, *weights_a, ids, scores = first_call(
        held, slots, section_table, route, route_x, score, score_x, whole_x, norm_gain, gain_x, own
    )
    out_a, out_b = [], []
    for step in range(stages):
        received = exchange(sent)
        if step == 0:
            made, weights = load_ffn(first_ffn_kernel, section_table, received, weights_a, other, True, 1)
            weights_a, weights_b = weights[:3], weights[3:]
        elif step in KEPT:
            made = ffn(step, section_table, received, weights_a)
        else:
            kernel = functools.partial(later_ffn_kernel, step)
            made, weights_a = load_ffn(kernel, section_table, received, weights_a, other, True)
        hidden, sent = small_call(
            between_kernel, "mix_norm_pack", (held, slots), (held,), (ids, scores), (hidden, exchange(made), gains)
        )
        out_a.append(hidden)
        received = exchange(sent)
        if step == 0:
            made, weights_b = load_ffn(second_ffn_kernel, section_table, received, weights_b, own, False)
        else:
            kernel = functools.partial(later_ffn_kernel, step)
            made, weights_b = load_ffn(kernel, section_table, received, weights_b, own, False)
        back = exchange(made)
        if step == stages - 1:
            break
        hidden = small_call(leave_kernel, "mix", (held,), (), (ids, scores), (hidden, back))
        out_b.append(hidden)
        hidden = lax.ppermute(hidden, "pipe", relay_pairs(step, stages))
        sent = small_call(enter_kernel, "norm_pack", (slots,), (held,), (ids,), (hidden, gains))

    kept, leaving = finish(section_table, ids, scores, hidden, back, out_a + out_b)
    whole = join(section_table, kept, swapped(leaving))
    return whole.reshape(1, 1, blocks * rows, width)


def solution(mesh):
    in_specs = (
        P(None, "expert", None),
        P("pipe", None),
        P("pipe", "expert", None, None),
        P("pipe", "expert", None, None),
        P("pipe", "expert", None, None),
        P("pipe", None, "expert", None),
        P("pipe", None, "expert", None),
    )
    out_specs = P("pipe", None, "expert", None)
    return jax.shard_map(shards, mesh=mesh, in_specs=in_specs, out_specs=out_specs, check_vma=False)
```

```python
import functools

import jax
import jax.numpy as jnp
from jax import lax
from jax.experimental import pallas as pl
from jax.experimental.pallas import tpu as pltpu
from jax.sharding import PartitionSpec as P

H_CUT = 256
D_CUT = 512
AHEAD = 10
KEPT = (1,)
K_CUT = 512
DOWN_PARTS = 3
SMALL = pltpu.CompilerParams(vmem_limit_bytes=8 * 1024 * 1024)


def in_vmem(x):
    return pltpu.with_memory_space_constraint(x, pltpu.VMEM)


def in_hbm(x):
    return pltpu.with_memory_space_constraint(x, pltpu.HBM)


def spec(space):
    return pl.BlockSpec(memory_space=space)


def core_of(section_ref):
    return section_ref[0] & 1


def working(section_ref, step):
    return (section_ref[0] >> 1) == step


def normalised(hidden, gain_row):
    scaled = lax.rsqrt(jnp.mean(hidden * hidden, axis=-1, keepdims=True) + 1e-06)
    return (hidden * scaled * gain_row).astype(jnp.bfloat16)


def mixed(which, ids_ref, scores_ref, hidden_ref, returned_ref, block):
    topk = ids_ref.shape[1]
    parts = [scores_ref[which, k, block] for k in range(topk)]
    whole = parts[0]
    for k in range(1, topk):
        whole = whole + parts[k]
    total = None
    for k in range(topk):
        weight = jnp.full((1, 1), parts[k], jnp.float32) / jnp.full((1, 1), whole, jnp.float32)
        term = returned_ref[ids_ref[which, k, block]].astype(jnp.float32) * weight
        total = term if total is None else total + term
    return (hidden_ref[block].astype(jnp.float32) + total).astype(jnp.bfloat16)


def pack(ids, normed_ref, packed_ref):
    for expert in range(packed_ref.shape[0]):
        block = jnp.int32(0)
        for b in range(1, len(ids)):
            for one in ids[b]:
                block = jnp.where(one == expert, jnp.int32(b), block)
        packed_ref[expert] = normed_ref[block]


def table_ids(which, ids_ref):
    topk, blocks = ids_ref.shape[1:]
    return [[ids_ref[which, k, b] for k in range(topk)] for b in range(blocks)]


def first_kernel(
    section_ref, rx_h, sx_h, gx, ro_h, so_h, go, x_hbm, gate, up, down,
    hidden_ref, packed_ref, gains_ref, gate_v, up_v, down_v, ids_ref, scores_ref,
    ro, rx, so, sx, normed_ref, gain_v, sems, weight_sems,
):
    core = core_of(section_ref)
    first = core == 0
    pairs = (
        (ro_h, ro), (rx_h, rx), (so_h, so), (sx_h, sx),
        (go, gain_v.at[0]), (gx, gain_v.at[1]), (x_hbm.at[:, core], hidden_ref),
    )
    copies = [pltpu.make_async_copy(source, target, sems.at[i]) for i, (source, target) in enumerate(pairs)]
    for copy in copies:
        copy.start()
    for copy in copies:
        copy.wait()
    loads = [
        pltpu.make_async_copy(source, target, weight_sems.at[i])
        for i, (source, target) in enumerate(((gate, gate_v), (up, up_v), (down, down_v)))
    ]

    topk, blocks = ro.shape
    ids = [[None] * topk for _ in range(blocks)]
    for b in range(blocks):
        for k in range(topk):
            ids[b][k] = jnp.where(first, ro[k, b], rx[k, b])
            ids_ref[0, k, b] = ids[b][k]
            ids_ref[1, k, b] = jnp.where(first, rx[k, b], ro[k, b])
            scores_ref[0, k, b] = jnp.where(first, so[k, b], sx[k, b])
            scores_ref[1, k, b] = jnp.where(first, sx[k, b], so[k, b])
    own = gain_v[0].astype(jnp.float32)
    other = gain_v[1].astype(jnp.float32)
    gain = jnp.where(first, own, other)
    gains_ref[0] = gain
    gains_ref[1] = jnp.where(first, other, own)
    for block in range(hidden_ref.shape[0]):
        normed_ref[block] = normalised(hidden_ref[block].astype(jnp.float32), gain)
    pack(ids, normed_ref, packed_ref)

    @pl.when(first)
    def _():
        for copy in loads:
            copy.start()
        for copy in loads:
            copy.wait()


def first_call(held, slots, section_table, route, route_x, score, score_x, whole_x, gain, gain_x, own):
    width = held[2]
    both = (2,) + route.shape
    return pl.pallas_call(
        first_kernel,
        out_shape=(
            pltpu.VMEM(held, jnp.bfloat16),
            pltpu.VMEM(slots, jnp.bfloat16),
            pltpu.VMEM((2, 1, width), jnp.float32),
            *[pltpu.VMEM(w.shape, w.dtype) for w in own],
            pltpu.SMEM(both, jnp.int32),
            pltpu.SMEM(both, jnp.float32),
        ),
        in_specs=[spec(pltpu.SMEM)] + [spec(pl.ANY)] * 3 + [spec(pltpu.HBM)] * 7,
        out_specs=(spec(pltpu.VMEM),) * 6 + (spec(pltpu.SMEM),) * 2,
        scratch_shapes=[
            pltpu.SMEM(route.shape, jnp.int32),
            pltpu.SMEM(route.shape, jnp.int32),
            pltpu.SMEM(route.shape, jnp.float32),
            pltpu.SMEM(route.shape, jnp.float32),
            pltpu.VMEM(held, jnp.bfloat16),
            pltpu.VMEM((2, 1, width), jnp.bfloat16),
            pltpu.SemaphoreType.DMA((7,)),
            pltpu.SemaphoreType.DMA((3,)),
        ],
        compiler_params=SMALL,
        name="slice_norm_pack",
    )(section_table, route_x, score_x, gain_x, *[in_hbm(v) for v in (route, score, gain, whole_x, *own)])


def enter_kernel(ids_ref, hidden_ref, gains_ref, packed_ref, normed_ref):
    for block in range(hidden_ref.shape[0]):
        normed_ref[block] = normalised(hidden_ref[block].astype(jnp.float32), gains_ref[0])
    pack(table_ids(0, ids_ref), normed_ref, packed_ref)


def between_kernel(ids_ref, scores_ref, hidden_ref, returned_ref, gains_ref, out_ref, packed_ref, normed_ref):
    for block in range(hidden_ref.shape[0]):
        result = mixed(0, ids_ref, scores_ref, hidden_ref, returned_ref, block)
        out_ref[block] = result
        normed_ref[block] = normalised(result.astype(jnp.float32), gains_ref[1])
    pack(table_ids(1, ids_ref), normed_ref, packed_ref)


def leave_kernel(ids_ref, scores_ref, hidden_ref, returned_ref, out_ref):
    for block in range(hidden_ref.shape[0]):
        out_ref[block] = mixed(1, ids_ref, scores_ref, hidden_ref, returned_ref, block)


def finish_kernel(section_ref, ids_ref, scores_ref, hidden_ref, returned_ref, *refs):
    earlier, (kept_ref, sent_ref, sems) = refs[:-3], refs[-3:]
    stages = (len(earlier) + 1) // 2
    last = stages - 1
    results_a, results_b = earlier[:stages], earlier[stages:]
    ways = ((0, (kept_ref, sent_ref)), (1, (sent_ref, kept_ref)))
    for step in range(stages):
        for core, (target_a, target_b) in ways:

            @pl.when(section_ref[0] == 2 * step + core)
            def _():
                pltpu.make_async_copy(results_a[step], target_a, sems.at[0]).start()
                if step < last:
                    pltpu.make_async_copy(results_b[step], target_b, sems.at[1]).start()
                else:
                    for block in range(hidden_ref.shape[0]):
                        target_b[block] = mixed(1, ids_ref, scores_ref, hidden_ref, returned_ref, block)

    pltpu.make_async_copy(results_a[0], kept_ref, sems.at[0]).wait()

    @pl.when(section_ref[0] < 2 * last)
    def _():
        pltpu.make_async_copy(results_a[0], sent_ref, sems.at[1]).wait()


def finish(section_table, ids, scores, hidden, returned, earlier):
    held = hidden.shape
    return pl.pallas_call(
        finish_kernel,
        out_shape=(pltpu.VMEM(held, jnp.bfloat16),) * 2,
        in_specs=[spec(pltpu.SMEM)] * 3 + [spec(pltpu.VMEM)] * 2 + [spec(pl.ANY)] * len(earlier),
        out_specs=(spec(pltpu.VMEM),) * 2,
        scratch_shapes=[pltpu.SemaphoreType.DMA((2,))],
        compiler_params=SMALL,
        name="mix_choose",
    )(section_table, ids, scores, in_vmem(hidden), in_vmem(returned), *earlier)


def join_kernel(section_ref, kept_ref, got_ref, out_ref, sems):
    lane = core_of(section_ref)
    copies = [
        pltpu.make_async_copy(kept_ref, out_ref.at[:, lane], sems.at[0]),
        pltpu.make_async_copy(got_ref, out_ref.at[:, 1 - lane], sems.at[1]),
    ]
    for copy in copies:
        copy.start()
    for copy in copies:
        copy.wait()


def join(section_table, kept, got):
    blocks, lane, width = kept.shape
    return pl.pallas_call(
        join_kernel,
        out_shape=pltpu.HBM((blocks, 2, lane, width), jnp.bfloat16),
        in_specs=[spec(pltpu.SMEM)] + [spec(pltpu.VMEM)] * 2,
        out_specs=spec(pltpu.HBM),
        scratch_shapes=[pltpu.SemaphoreType.DMA((2,))],
        compiler_params=SMALL,
        name="join_rows",
    )(section_table, in_vmem(kept), in_vmem(got))


def small_call(kernel, name, outs, scratch, smem, vmem):
    single = len(outs) == 1
    shapes = tuple(pltpu.VMEM(o, jnp.bfloat16) for o in outs)
    specs = tuple(spec(pltpu.VMEM) for _ in outs)
    return pl.pallas_call(
        kernel,
        out_shape=shapes[0] if single else shapes,
        in_specs=[spec(pltpu.SMEM)] * len(smem) + [spec(pltpu.VMEM)] * len(vmem),
        out_specs=specs[0] if single else specs,
        scratch_shapes=[pltpu.VMEM(s, jnp.bfloat16) for s in scratch],
        compiler_params=SMALL,
        name=name,
    )(*smem, *[in_vmem(v) for v in vmem])


def silu_times(gate_part, up_part):
    return (gate_part / (1.0 + jnp.exp(-gate_part)) * up_part).astype(jnp.bfloat16)


def down_part(active_v, down_ref, out_ref):
    for c in range(down_ref.shape[1] // D_CUT):
        cut = pl.ds(c * D_CUT, D_CUT)
        produced = jnp.dot(active_v[...], down_ref[:, cut], preferred_element_type=jnp.float32)
        out_ref[:, cut] = produced.astype(jnp.bfloat16)


def load_copies(sources, targets, sems):
    (gate, up, down), (gate_ref, up_ref, down_ref) = sources, targets
    parts = gate_ref.shape[0] // K_CUT
    down_rows = down_ref.shape[0] // DOWN_PARTS
    made = []
    for c in range(parts):
        cut = pl.ds(c * K_CUT, K_CUT)
        made.append(pltpu.make_async_copy(gate.at[cut], gate_ref.at[cut], sems.at[2 * c]))
        made.append(pltpu.make_async_copy(up.at[cut], up_ref.at[cut], sems.at[2 * c + 1]))
    for c in range(DOWN_PARTS):
        cut = pl.ds(c * down_rows, down_rows)
        made.append(pltpu.make_async_copy(down.at[cut], down_ref.at[cut], sems.at[2 * parts + c]))
    return made


def streamed_ffn(x_ref, targets, out_ref, active_v, gate_sum, up_sum, down_sum, ready):
    gate_ref, up_ref, down_ref = targets
    parts = gate_ref.shape[0] // K_CUT
    for c in range(parts):
        cut = pl.ds(c * K_CUT, K_CUT)
        for i, weight_ref, sum_ref in ((2 * c, gate_ref, gate_sum), (2 * c + 1, up_ref, up_sum)):
            ready(i)
            term = jnp.dot(x_ref[:, cut], weight_ref[cut, :], preferred_element_type=jnp.float32)
            sum_ref[...] = term if c == 0 else sum_ref[...] + term
    active_v[...] = silu_times(gate_sum[...], up_sum[...])
    down_rows = down_ref.shape[0] // DOWN_PARTS
    for c in range(DOWN_PARTS):
        ready(2 * parts + c)
        cut = pl.ds(c * down_rows, down_rows)
        term = jnp.dot(active_v[:, cut], down_ref[cut, :], preferred_element_type=jnp.float32)
        if c == 0:
            down_sum[...] = term
        elif c < DOWN_PARTS - 1:
            down_sum[...] += term
        else:
            out_ref[...] = (down_sum[...] + term).astype(jnp.bfloat16)


def first_ffn_kernel(
    section_ref, x_ref, gi, ui, di, gx, ux, dx, out_ref, gate_ref, up_ref, down_ref, gate_next, up_next, down_next,
    active_v, gate_sum, up_sum, down_sum, sems
):
    targets = (gate_ref, up_ref, down_ref)

    @pl.when(core_of(section_ref) == 0)
    def _():
        copies = load_copies((gx, ux, dx), (gate_next, up_next, down_next), sems)
        for copy in copies:
            copy.start()
        for copy in copies[:AHEAD]:
            copy.wait()

        @pl.when(working(section_ref, 0))
        def _():
            ffn_body(x_ref, *targets, out_ref, active_v)

        for copy in copies[AHEAD:]:
            copy.wait()

    @pl.when(core_of(section_ref) != 0)
    def _():
        stream_and_run(section_ref, x_ref, (gx, ux, dx), targets, out_ref, active_v, gate_sum, up_sum, down_sum, sems)


def stream_and_run(section_ref, x_ref, sources, targets, out_ref, active_v, gate_sum, up_sum, down_sum, sems):
    copies = load_copies(sources, targets, sems)
    for copy in copies:
        copy.start()

    @pl.when(working(section_ref, 0))
    def _():
        streamed_ffn(x_ref, targets, out_ref, active_v, gate_sum, up_sum, down_sum, lambda i: copies[i].wait())

    @pl.when(jnp.logical_not(working(section_ref, 0)))
    def _():
        for copy in copies:
            copy.wait()


def second_ffn_kernel(
    section_ref, x_ref, gi, ui, di, g_h, u_h, d_h, out_ref, gate_ref, up_ref, down_ref,
    active_v, gate_sum, up_sum, down_sum, sems
):
    targets = (gate_ref, up_ref, down_ref)

    @pl.when(jnp.logical_and(core_of(section_ref) == 0, working(section_ref, 0)))
    def _():
        ffn_body(x_ref, *targets, out_ref, active_v)

    @pl.when(core_of(section_ref) != 0)
    def _():
        stream_and_run(section_ref, x_ref, (g_h, u_h, d_h), targets, out_ref, active_v, gate_sum, up_sum, down_sum, sems)


def later_ffn_kernel(
    step, section_ref, x_ref, gi, ui, di, g_h, u_h, d_h, out_ref, gate_ref, up_ref, down_ref,
    active_v, gate_sum, up_sum, down_sum, sems
):
    @pl.when(core_of(section_ref) != 0)
    def _():
        copies = load_copies((g_h, u_h, d_h), (gate_ref, up_ref, down_ref), sems)
        for copy in copies:
            copy.start()
        for copy in copies:
            copy.wait()

    @pl.when(working(section_ref, step))
    def _():
        ffn_body(x_ref, gate_ref, up_ref, down_ref, out_ref, active_v)


def ffn_cost(flat, hidden):
    rows, width = flat.shape
    return pl.CostEstimate(
        flops=6 * rows * width * hidden,
        bytes_accessed=6 * width * hidden + 4 * rows * width,
        transcendentals=rows * hidden,
    )


def load_ffn(kernel, section_table, received, present, sources, anywhere, extra=0):
    experts, rows, width = received.shape
    hidden = present[0].shape[1]
    flat = received.reshape(experts * rows, width)
    sums = pltpu.VMEM((flat.shape[0], hidden), jnp.float32)
    produced, *weights = pl.pallas_call(
        kernel,
        out_shape=(
            pltpu.VMEM(flat.shape, jnp.bfloat16),
            *[pltpu.VMEM(w.shape, w.dtype) for w in present] * (1 + extra),
        ),
        in_specs=[spec(pltpu.SMEM)] + [spec(pltpu.VMEM)] * 4 + [spec(pl.ANY if anywhere else pltpu.HBM)] * 3,
        out_specs=(spec(pltpu.VMEM),) * (4 + 3 * extra),
        scratch_shapes=[
            pltpu.VMEM((flat.shape[0], hidden), jnp.bfloat16),
            sums,
            sums,
            pltpu.VMEM(flat.shape, jnp.float32),
            pltpu.SemaphoreType.DMA((2 * (width // K_CUT) + DOWN_PARTS,)),
        ],
        input_output_aliases={2: 1, 3: 2, 4: 3},
        compiler_params=SMALL,
        cost_estimate=ffn_cost(flat, hidden),
        name="load_expert_ffn",
    )(
        section_table,
        in_vmem(flat),
        *[in_vmem(w) for w in present],
        *(sources if anywhere else [in_hbm(w) for w in sources]),
    )
    return produced.reshape(received.shape), weights


def ffn_body(x_ref, gate_ref, up_ref, down_ref, out_ref, active_v):
    for c in range(gate_ref.shape[1] // H_CUT):
        cut = pl.ds(c * H_CUT, H_CUT)
        gate_part = jnp.dot(x_ref[...], gate_ref[:, cut], preferred_element_type=jnp.float32)
        up_part = jnp.dot(x_ref[...], up_ref[:, cut], preferred_element_type=jnp.float32)
        active_v[:, cut] = silu_times(gate_part, up_part)
    down_part(active_v, down_ref, out_ref)


def ffn_kernel(step, section_ref, x_ref, gate_ref, up_ref, down_ref, out_ref, active_v):
    @pl.when(working(section_ref, step))
    def _():
        ffn_body(x_ref, gate_ref, up_ref, down_ref, out_ref, active_v)


def ffn(step, section_table, received, weights):
    experts, rows, width = received.shape
    flat = received.reshape(experts * rows, width)
    hidden = weights[0].shape[1]
    produced = pl.pallas_call(
        functools.partial(ffn_kernel, step),
        out_shape=pltpu.VMEM(flat.shape, jnp.bfloat16),
        in_specs=[spec(pltpu.SMEM)] + [spec(pltpu.VMEM)] * 4,
        out_specs=spec(pltpu.VMEM),
        scratch_shapes=[pltpu.VMEM((flat.shape[0], hidden), jnp.bfloat16)],
        compiler_params=SMALL,
        cost_estimate=ffn_cost(flat, hidden),
        name="expert_ffn",
    )(section_table, in_vmem(flat), *[in_vmem(w) for w in weights])
    return produced.reshape(received.shape)


def exchange(slots):
    return lax.all_to_all(slots, "expert", 0, 0, tiled=True)


def relay_pairs(step, stages):
    place = list(range(stages))
    for x in range(step % 2, stages - 1, 2):
        place[x], place[x + 1] = x + 1, x
    if step % 2:
        place[0], place[-1] = stages - 1, 0
    return [(2 * x + c, 2 * place[x] + c) for x in range(stages) for c in range(2)]


def shards(activations, norm_gain, w_gate, w_up, w_down, routes, gate_scores):
    sections = lax.axis_size("pipe")
    experts = lax.axis_size("expert")
    section = lax.axis_index("pipe")
    stages = sections // 2
    blocks, topk = routes.shape[2:]
    rows = activations.shape[1] // blocks
    lane = rows // 2
    width = activations.shape[2]
    held = (blocks, lane, width)
    slots = (experts, lane, width)
    swap = [(i, i ^ 1) for i in range(sections)]

    def swapped(x):
        return lax.ppermute(x, "pipe", swap)

    route = routes[0, 0].T
    score = gate_scores[0, 0].T
    route_x, gain_x, score_x = swapped(route), swapped(norm_gain), swapped(score)
    own = (w_gate[0, 0], w_up[0, 0], w_down[0, 0])
    *own, route_x, gain_x, score_x = lax.optimization_barrier((*own, route_x, gain_x, score_x))
    other = tuple(swapped(w) for w in own)
    section_table = section.astype(jnp.int32).reshape(1)

    whole_x = activations[0].reshape(blocks, 2, lane, width)
    hidden, sent, gains, *weights_a, ids, scores = first_call(
        held, slots, section_table, route, route_x, score, score_x, whole_x, norm_gain, gain_x, own
    )
    out_a, out_b = [], []
    for step in range(stages):
        received = exchange(sent)
        if step == 0:
            made, weights = load_ffn(first_ffn_kernel, section_table, received, weights_a, other, True, 1)
            weights_a, weights_b = weights[:3], weights[3:]
        elif step in KEPT:
            made = ffn(step, section_table, received, weights_a)
        else:
            kernel = functools.partial(later_ffn_kernel, step)
            made, weights_a = load_ffn(kernel, section_table, received, weights_a, other, True)
        hidden, sent = small_call(
            between_kernel, "mix_norm_pack", (held, slots), (held,), (ids, scores), (hidden, exchange(made), gains)
        )
        out_a.append(hidden)
        received = exchange(sent)
        if step == 0:
            made, weights_b = load_ffn(second_ffn_kernel, section_table, received, weights_b, own, False)
        else:
            kernel = functools.partial(later_ffn_kernel, step)
            made, weights_b = load_ffn(kernel, section_table, received, weights_b, own, False)
        back = exchange(made)
        if step == stages - 1:
            break
        hidden = small_call(leave_kernel, "mix", (held,), (), (ids, scores), (hidden, back))
        out_b.append(hidden)
        hidden = lax.ppermute(hidden, "pipe", relay_pairs(step, stages))
        sent = small_call(enter_kernel, "norm_pack", (slots,), (held,), (ids,), (hidden, gains))

    kept, leaving = finish(section_table, ids, scores, hidden, back, out_a + out_b)
    whole = join(section_table, kept, swapped(leaving))
    return whole.reshape(1, 1, blocks * rows, width)


def solution(mesh):
    in_specs = (
        P(None, "expert", None),
        P("pipe", None),
        P("pipe", "expert", None, None),
        P("pipe", "expert", None, None),
        P("pipe", "expert", None, None),
        P("pipe", None, "expert", None),
        P("pipe", None, "expert", None),
    )
    out_specs = P("pipe", None, "expert", None)
    return jax.shard_map(shards, mesh=mesh, in_specs=in_specs, out_specs=out_specs, check_vma=False)
```
